32 devices in a mesh: sub: 8 (over z, y), slab: 4 (over x, core).
Axes of the slice: x: 2, y: 2, z: 4, core: 2. Of those that a mesh axis runs over, the one named last changes fastest.
Arguments:
- mode_shapes: bfloat16 [8, 256, 64], P('sub', 'slab'), may hold values from -0.375 to 0.375
- coupling_k: bfloat16 [8, 256, 1024], P('sub', 'slab'), may hold values from -1 to 1
- coupling_m: bfloat16 [8, 256, 1024], P('sub', 'slab'), may hold values from -1 to 1
- tile_range: int32 [8, 2, 8], P('sub'), may hold values from 0 to 256, as said below
- eigenvalues: float32 [8, 64], P('sub'), may hold values from 0.5 to 8
- adjacency: int32 [8, 8], replicated, may hold values from 0 to 15, as said below
- piece_slot: int32 [16], replicated, may hold values from 0 to 15, as said below
- interface_k: float32 [16, 128, 128], P('sub', 'slab'), may hold values from -0.3 to 0.3
- interface_m: float32 [16, 128, 128], P('sub', 'slab'), may hold values from -0.3 to 0.3
Outputs:
- reduced_k: float32 [16, 128, 128], P('sub', 'slab')
- reduced_m: float32 [16, 128, 128], P('sub', 'slab')
The draws below stay inside these ranges and needn't reach their ends.
Inputs may be any that keep to these rules, and one draw needn't show every extreme that they name: `adjacency`: each piece's owner device is piece_slot[p] // 2. The 8 pieces of one row have 8 different owner devices, and one owner device is adjacent to every substructure. `piece_slot`: each output row holds exactly one piece. tile_range[i, 0, a] < tile_range[i, 1, a].
All inputs are finite; a program needn't handle non-finite values.
Results may differ from the reference program's by a relative error of at most 0.0034.
Values may be sent and summed in bfloat16 or wider, within the bound.
A program may use at most 64 MiB of HBM per device.

```python
import math
import jax
import jax.numpy as jnp
from jax import lax

MODES = 64
PIECE_W = 128
TILE_ROWS = 256
PIECE_DEV = 2
NSUBS = 8
ADJ = 8
NP = 16


def joint_routing(key):
    key_perm = jax.random.fold_in(key, 101)
    key_center = jax.random.fold_in(key, 202)
    key_scores = jax.random.fold_in(key, 303)
    key_local = jax.random.fold_in(key, 404)
    owners_total = NP // PIECE_DEV
    permuted = jax.random.permutation(key_perm, NP).astype(jnp.int32)
    inverse = jnp.argsort(permuted).astype(jnp.int32)
    center = jax.random.randint(key_center, (), 0, owners_total)
    column = lax.iota(jnp.int32, owners_total)
    scores = jax.random.randint(key_scores, (NSUBS, owners_total), 0, 1 << 16) * owners_total + column[None, :]
    scores = jnp.where(column[None, :] == center, -1, scores)
    owners = jnp.argsort(scores, axis=1)[:, :ADJ].astype(jnp.int32)
    local_slot = jax.random.randint(key_local, (NSUBS, ADJ), 0, PIECE_DEV)
    slots = owners * PIECE_DEV + local_slot
    return (inverse[slots].astype(jnp.int32), permuted)


def draw_adjacency(key, part):
    return joint_routing(key)[0]


def draw_piece_slot(key, part):
    return joint_routing(key)[1]


def draw_tile_range(key, part):
    key_start = jax.random.fold_in(key, 11)
    key_length = jax.random.fold_in(key, 22)
    start = jax.random.randint(key_start, (NSUBS, ADJ), 0, TILE_ROWS // 2)
    length = jax.random.randint(key_length, (NSUBS, ADJ), TILE_ROWS // 4 + 1, TILE_ROWS - start + 1)
    finish = start + length
    column = lax.iota(jnp.int32, ADJ)[None, :]
    start = jnp.where(column == 1, 0, start)
    finish = jnp.where(column == 0, TILE_ROWS, finish)
    return jnp.stack([start, finish], axis=1).astype(jnp.int32)


def block_levels(key, dims, split, smallest, top_value):
    def one(axis_at, parts):
        heights = jax.random.uniform(jax.random.fold_in(jax.random.fold_in(key, 6), axis_at), (parts,), jnp.float32, smallest / len(split), top_value / len(split))
        return jnp.repeat(jnp.exp(heights), dims[axis_at] // parts).reshape((-1,) + (1,) * (len(dims) - axis_at - 1))

    loudness = one(*split[0])
    for cut in split[1:]:
        loudness = loudness * one(*cut)
    return loudness


def scatter_about(key, extent, width, most, cuts=(), dtype=jnp.bfloat16):
    level = block_levels(key, extent, cuts, -0.22, 0.18) if cuts else 1.0
    entries = jax.random.normal(key, extent, jnp.float32) * width * level
    return jnp.minimum(jnp.maximum(entries, -most), most).astype(dtype)


def setup_inputs(seed: int = 0) -> dict:
    key_of = jax.random.split(jax.random.key(seed), 10)
    mode_shapes = scatter_about(key_of[0], (NSUBS, TILE_ROWS, MODES), TILE_ROWS ** -0.5, 0.375, ((0, 8), (1, 4)))
    coupling_k = scatter_about(key_of[1], (NSUBS, TILE_ROWS, ADJ * PIECE_W), 0.125, 1.0, ((0, 8), (1, 4)))
    coupling_m = scatter_about(key_of[2], (NSUBS, TILE_ROWS, ADJ * PIECE_W), 0.125, 1.0, ((0, 8), (1, 4)))
    tile_range = draw_tile_range(jax.random.fold_in(key_of[9], 71), 0)
    eigenvalues = jnp.clip(jnp.exp(math.log(8.0) - 2.7725887 * jax.random.uniform(key_of[4], (NSUBS, MODES), jnp.float32) ** block_levels(key_of[4], (NSUBS, MODES), ((0, 8),), -0.2, 0.2)), 0.5, 8.0)
    adjacency = draw_adjacency(jax.random.fold_in(key_of[9], 71), 0)
    piece_slot = draw_piece_slot(jax.random.fold_in(key_of[9], 71), 0)
    interface_k = scatter_about(key_of[7], (NP, PIECE_W, PIECE_W), 0.05, 0.3, ((0, 8), (1, 4)), jnp.float32)
    interface_m = scatter_about(key_of[8], (NP, PIECE_W, PIECE_W), 0.05, 0.3, ((0, 8), (1, 4)), jnp.float32)
    return dict(mode_shapes=mode_shapes, coupling_k=coupling_k, coupling_m=coupling_m, tile_range=tile_range, eigenvalues=eigenvalues, adjacency=adjacency, piece_slot=piece_slot, interface_k=interface_k, interface_m=interface_m)


def reference(mode_shapes, coupling_k, coupling_m, tile_range, eigenvalues, adjacency, piece_slot, interface_k, interface_m):
    row_index = lax.iota(jnp.int32, TILE_ROWS)

    def factors(sub_idx):
        start = tile_range[sub_idx, 0]
        finish = tile_range[sub_idx, 1]
        live = ((row_index[:, None] >= start[None, :]) & (row_index[:, None] < finish[None, :])).astype(jnp.bfloat16)
        stiff_rows = (coupling_k[sub_idx].reshape(TILE_ROWS, ADJ, PIECE_W) * live[:, :, None]).reshape(TILE_ROWS, ADJ * PIECE_W)
        mass_rows = (coupling_m[sub_idx].reshape(TILE_ROWS, ADJ, PIECE_W) * live[:, :, None]).reshape(TILE_ROWS, ADJ * PIECE_W)
        proj_s = jnp.dot(mode_shapes[sub_idx].T, stiff_rows, preferred_element_type=jnp.float32)
        proj_v = jnp.dot(mode_shapes[sub_idx].T, mass_rows, preferred_element_type=jnp.float32)
        eig_vals = eigenvalues[sub_idx][:, None]
        first = (proj_s * lax.rsqrt(eig_vals)).astype(jnp.bfloat16)
        second = (proj_s / eig_vals - proj_v).astype(jnp.bfloat16)
        third = proj_v.astype(jnp.bfloat16)
        return jnp.stack([first, second, third]).reshape(3, MODES, ADJ, PIECE_W)
    stacked = lax.map(factors, lax.iota(jnp.int32, NSUBS))

    def accumulate(carry, sub_idx):
        gram_k, gram_m = carry
        local = stacked[sub_idx].astype(jnp.float32)
        slots = piece_slot[adjacency[sub_idx]].astype(jnp.int32)
        hp = lax.Precision.HIGHEST
        term_k = jnp.einsum('mab,mac->abc', local[0], local[0], precision=hp)
        term_m = jnp.einsum('mab,mac->abc', local[1], local[1], precision=hp) - jnp.einsum('mab,mac->abc', local[2], local[2], precision=hp)
        return ((gram_k.at[slots].add(term_k), gram_m.at[slots].add(term_m)), None)
    zeros = jnp.zeros((NP, PIECE_W, PIECE_W), jnp.float32)
    (gram_k, gram_m), _ = lax.scan(accumulate, (zeros, zeros), lax.iota(jnp.int32, NSUBS))
    return (interface_k + gram_k, interface_m + gram_m)
```

```python
import functools

import jax
import jax.numpy as jnp
from jax import lax
from jax.experimental import pallas as pl
from jax.experimental.pallas import tpu as pltpu
from jax.sharding import PartitionSpec as P

MESH = pl.DeviceIdType.MESH


def contract_rows(left, right):
    return lax.dot_general(
        left, right, (((0,), (0,)), ((), ())), preferred_element_type=jnp.float32
    )


def kernel(
    subs,
    slabs,
    adjacency,
    piece_slot,
    tile_range,
    eigenvalues,
    modes,
    coupling_k,
    coupling_m,
    interface_k,
    interface_m,
    reduced_k,
    reduced_m,
    tile_k,
    tile_m,
    outgoing,
    columns,
    all_modes,
    blocks,
    arrived,
    local_sem,
    modes_send,
    modes_recv,
    columns_send,
    columns_recv,
    blocks_send,
    blocks_recv,
):
    sub = lax.axis_index("sub")
    slab = lax.axis_index("slab")
    group = subs // slabs
    adj = adjacency.shape[1]
    owned, quarter, width = interface_k.shape
    rows = modes.shape[1]
    home = sub // group

    loads = [
        pltpu.make_async_copy(
            whole.at[0, :, a * width : (a + 1) * width], tile.at[a], local_sem.at[kind, a]
        )
        for a in range(adj)
        for kind, (whole, tile) in enumerate(((coupling_k, tile_k), (coupling_m, tile_m)))
    ]
    loads.append(pltpu.make_async_copy(modes.at[0], all_modes.at[slab], modes_recv.at[slab]))
    for load in loads:
        load.start()

    barrier = pltpu.get_barrier_semaphore()
    for turn in range(1, slabs):
        pl.semaphore_signal(
            barrier, inc=1, device_id=(sub, lax.rem(slab + turn, slabs)), device_id_type=MESH
        )
    for turn in range(1, subs):
        pl.semaphore_signal(
            barrier, inc=1, device_id=(lax.rem(sub + turn, subs), home), device_id_type=MESH
        )

    @pl.when(home != slab)
    def _():
        pl.semaphore_signal(barrier, inc=1, device_id=(sub, home), device_id_type=MESH)

    slots = [piece_slot[adjacency[sub, a]] for a in range(adj)]

    def owner_of(part, step):
        return part * group + lax.rem(step + sub + 1, group)

    for load in loads[:-1]:
        load.wait()
    row_index = slab * rows + lax.broadcasted_iota(jnp.int32, (rows, width), 0)
    for turn in list(range(1, slabs)) + [0]:
        part = lax.rem(slab + turn, slabs)
        for step in range(group):
            owner = owner_of(part, step)
            place = jnp.int32(0)
            for a in range(adj):
                mine = (slots[a] >= owner * owned) & (slots[a] < (owner + 1) * owned)
                place = jnp.where(mine, jnp.int32(a), place)
            start = tile_range[0, 0, place]
            finish = tile_range[0, 1, place]
            live = ((row_index >= start) & (row_index < finish)).astype(jnp.float32)
            live = live.astype(jnp.bfloat16)
            stiff = tile_k[place] * live
            mass = tile_m[place] * live
            if turn == 0:
                columns[step, slab, :, 0:width] = stiff
                columns[step, slab, :, width:] = mass
            else:
                outgoing[step, turn - 1, :, 0:width] = stiff
                outgoing[step, turn - 1, :, width:] = mass

    @pl.when(home != slab)
    def _():
        pl.semaphore_wait(barrier, slabs - 1 + group * slabs)

    @pl.when(home == slab)
    def _():
        pl.semaphore_wait(barrier, slabs - 1 + group * slabs - 1)

    sends = []
    for turn in range(1, slabs):
        part = lax.rem(slab + turn, slabs)
        copy = pltpu.make_async_remote_copy(
            src_ref=modes.at[0],
            dst_ref=all_modes.at[slab],
            send_sem=modes_send.at[turn - 1],
            recv_sem=modes_recv.at[slab],
            device_id=(sub, part),
            device_id_type=MESH,
        )
        copy.start()
        sends.append(copy)
    for step in range(group):
        for turn in range(1, slabs):
            part = lax.rem(slab + turn, slabs)
            copy = pltpu.make_async_remote_copy(
                src_ref=outgoing.at[step, turn - 1],
                dst_ref=columns.at[step, slab],
                send_sem=columns_send.at[step, turn - 1],
                recv_sem=columns_recv.at[step, slab],
                device_id=(sub, part),
                device_id_type=MESH,
            )
            copy.start()
            sends.append(copy)

    takes = []
    for other in range(subs):
        theirs = [piece_slot[adjacency[other, a]] for a in range(adj)]
        takes.append([
            functools.reduce(
                lambda x, y: x | y,
                [(slot == sub * owned + q).astype(jnp.int32) for slot in theirs],
            )
            for q in range(owned)
        ])
    eig = jnp.broadcast_to(eigenvalues[...], (width, modes.shape[2])).T
    root = lax.rsqrt(eig)

    loads[-1].wait()
    for turn in range(1, slabs):
        part = lax.rem(slab + turn, slabs)
        pltpu.make_async_copy(all_modes.at[part], all_modes.at[part], modes_recv.at[part]).wait()
    basis = all_modes[...].reshape(slabs * rows, modes.shape[2])
    for step in range(group):
        for turn in range(1, slabs):
            part = lax.rem(slab + turn, slabs)
            pltpu.make_async_copy(
                columns.at[step, part], columns.at[step, part], columns_recv.at[step, part]
            ).wait()
        proj = contract_rows(basis, columns[step].reshape(slabs * rows, 2 * width))
        proj_s, proj_v = proj[:, :width], proj[:, width:]
        first = (proj_s * root).astype(jnp.bfloat16)
        second = (proj_s / eig - proj_v).astype(jnp.bfloat16)
        third = proj_v.astype(jnp.bfloat16)
        gram_k = contract_rows(first, first)
        gram_m = contract_rows(
            jnp.concatenate([second, third]), jnp.concatenate([second, -third])
        )
        blocks[step, :, 0] = gram_k.astype(jnp.bfloat16).reshape(slabs, quarter, width)
        blocks[step, :, 1] = gram_m.astype(jnp.bfloat16).reshape(slabs, quarter, width)
        owner = owner_of(slab, step)
        for turn in range(1, slabs + 1):
            part = lax.rem(slab + turn, slabs)
            copy = pltpu.make_async_remote_copy(
                src_ref=blocks.at[step, part],
                dst_ref=arrived.at[sub],
                send_sem=blocks_send.at[step, turn - 1],
                recv_sem=blocks_recv.at[sub],
                device_id=(owner, part),
                device_id_type=MESH,
            )
            if turn < slabs:
                copy.start()
                sends.append(copy)
            else:
                pl.when(owner != sub)(copy.start)

                @pl.when(owner == sub)
                def _():
                    arrived[sub] = blocks[step, slab]

    total = [[interface_k[q] for q in range(owned)], [interface_m[q] for q in range(owned)]]
    for other in range(subs):

        @pl.when((other != sub) | (home != slab))
        def _():
            pltpu.make_async_copy(
                arrived.at[other], arrived.at[other], blocks_recv.at[other]
            ).wait()

        for kind in range(2):
            term = arrived[other, kind].astype(jnp.float32)
            for q in range(owned):
                total[kind][q] = total[kind][q] + jnp.where(takes[other][q] > 0, term, 0.0)
    for q in range(owned):
        reduced_k[q] = total[0][q]
        reduced_m[q] = total[1][q]

    for copy in sends:
        copy.wait_send()
    for step in range(group):

        @pl.when(owner_of(slab, step) != sub)
        def _():
            pltpu.make_async_copy(
                blocks.at[step, slab], blocks.at[step, slab], blocks_send.at[step, slabs - 1]
            ).wait()


def dense_body(
    subs,
    slabs,
    mode_shapes,
    coupling_k,
    coupling_m,
    tile_range,
    eigenvalues,
    adjacency,
    piece_slot,
    interface_k,
    interface_m,
):
    _, rows, mode_count = mode_shapes.shape
    adj = adjacency.shape[1]
    owned, quarter, width = interface_k.shape
    group = subs // slabs
    vmem = pl.BlockSpec(memory_space=pltpu.VMEM)
    smem = pl.BlockSpec(memory_space=pltpu.SMEM)
    hbm = pl.BlockSpec(memory_space=pl.ANY)
    out = jax.ShapeDtypeStruct(interface_k.shape, interface_k.dtype)
    return pl.pallas_call(
        functools.partial(kernel, subs, slabs),
        out_shape=(out, out),
        in_specs=[smem, smem, smem, vmem, hbm, hbm, hbm, vmem, vmem],
        out_specs=(vmem, vmem),
        scratch_shapes=[
            pltpu.VMEM((adj, rows, width), jnp.bfloat16),
            pltpu.VMEM((adj, rows, width), jnp.bfloat16),
            pltpu.VMEM((group, slabs - 1, rows, 2 * width), jnp.bfloat16),
            pltpu.VMEM((group, slabs, rows, 2 * width), jnp.bfloat16),
            pltpu.VMEM((slabs, rows, mode_count), jnp.bfloat16),
            pltpu.VMEM((group, slabs, 2, quarter, width), jnp.bfloat16),
            pltpu.VMEM((subs, 2, quarter, width), jnp.bfloat16),
            pltpu.SemaphoreType.DMA((2, adj)),
            pltpu.SemaphoreType.DMA((slabs - 1,)),
            pltpu.SemaphoreType.DMA((slabs,)),
            pltpu.SemaphoreType.DMA((group, slabs - 1)),
            pltpu.SemaphoreType.DMA((group, slabs)),
            pltpu.SemaphoreType.DMA((group, slabs)),
            pltpu.SemaphoreType.DMA((subs,)),
        ],
        compiler_params=pltpu.CompilerParams(
            collective_id=0, has_side_effects=True, vmem_limit_bytes=16 * 1024 * 1024
        ),
    )(
        adjacency,
        piece_slot,
        tile_range,
        eigenvalues,
        mode_shapes,
        coupling_k,
        coupling_m,
        interface_k,
        interface_m,
    )


def sparse_body(
    mode_shapes,
    coupling_k,
    coupling_m,
    tile_range,
    eigenvalues,
    adjacency,
    piece_slot,
    interface_k,
    interface_m,
):
    row_count = mode_shapes.shape[1]
    mode_count = mode_shapes.shape[2]
    adj_count = adjacency.shape[1]
    piece_width = interface_k.shape[2]
    owned_count = interface_k.shape[0]
    quarter_rows = interface_k.shape[1]
    sub_count = lax.axis_size("sub")
    slab_pos = lax.axis_index("slab")
    sub_pos = lax.axis_index("sub")
    row_index = slab_pos * row_count + lax.iota(jnp.int32, row_count)
    live = (
        (row_index[:, None] >= tile_range[0, 0][None, :])
        & (row_index[:, None] < tile_range[0, 1][None, :])
    ).astype(jnp.bfloat16)
    stiff_rows = (
        coupling_k[0].reshape(row_count, adj_count, piece_width) * live[:, :, None]
    ).reshape(row_count, adj_count * piece_width)
    mass_rows = (
        coupling_m[0].reshape(row_count, adj_count, piece_width) * live[:, :, None]
    ).reshape(row_count, adj_count * piece_width)
    part_s = jnp.einsum("rm,rc->mc", mode_shapes[0], stiff_rows, preferred_element_type=jnp.float32)
    part_v = jnp.einsum("rm,rc->mc", mode_shapes[0], mass_rows, preferred_element_type=jnp.float32)
    proj_s, proj_v = lax.psum((part_s, part_v), "slab")
    eig_held = eigenvalues[0]
    eig_col = eig_held[:, None]
    first = (proj_s * lax.rsqrt(eig_col)).astype(jnp.bfloat16)
    second = (proj_s / eig_col - proj_v).astype(jnp.bfloat16)
    third = proj_v.astype(jnp.bfloat16)
    stacked = jnp.stack([first, second, third]).reshape(3, mode_count, adj_count, piece_width)
    my_slots = piece_slot[adjacency[sub_pos]]
    owner_hot = (
        my_slots[None, :] // owned_count == lax.iota(jnp.int32, sub_count)[:, None]
    ).astype(jnp.bfloat16)
    outgoing = jnp.einsum(
        "oa,kmab->okmb", owner_hot, stacked, preferred_element_type=jnp.float32
    ).astype(jnp.bfloat16)
    incoming = lax.all_to_all(outgoing, "sub", split_axis=0, concat_axis=0, tiled=True)
    all_slots = piece_slot[adjacency]
    targets = sub_pos * owned_count + lax.iota(jnp.int32, owned_count)
    select = jnp.any(all_slots[:, :, None] == targets[None, None, :], axis=1).astype(jnp.bfloat16)

    def piece_gram(weights):
        picked = incoming * weights[:, None, None, None]
        left_side = lax.dynamic_slice_in_dim(picked, slab_pos * quarter_rows, quarter_rows, 3)
        gram_stiff = jnp.einsum(
            "smb,smc->bc", left_side[:, 0], incoming[:, 0], preferred_element_type=jnp.float32
        )
        gram_mass = jnp.einsum(
            "smb,smc->bc", left_side[:, 1], incoming[:, 1], preferred_element_type=jnp.float32
        )
        gram_mass = gram_mass - jnp.einsum(
            "smb,smc->bc", left_side[:, 2], incoming[:, 2], preferred_element_type=jnp.float32
        )
        return (gram_stiff, gram_mass)

    gram_k, gram_m = lax.map(piece_gram, select.T)
    return (interface_k + gram_k, interface_m + gram_m)


def body(subs, slabs, *arrays):
    adjacency = arrays[5]
    if adjacency.shape[1] == subs and subs % slabs == 0:
        return dense_body(subs, slabs, *arrays)
    return sparse_body(*arrays)


def solution(mesh):
    placed = (
        P("sub", "slab", None),
        P("sub", "slab", None),
        P("sub", "slab", None),
        P("sub", None, None),
        P("sub", None),
        P(),
        P(),
        P("sub", "slab", None),
        P("sub", "slab", None),
    )
    return jax.shard_map(
        functools.partial(body, mesh.shape["sub"], mesh.shape["slab"]),
        mesh=mesh,
        in_specs=placed,
        out_specs=(P("sub", "slab", None), P("sub", "slab", None)),
        check_vma=False,
    )
```

```python
import functools

import jax
import jax.numpy as jnp
from jax import lax
from jax.experimental import pallas as pl
from jax.experimental.pallas import tpu as pltpu
from jax.sharding import PartitionSpec as P

MESH = pl.DeviceIdType.MESH


def contract_rows(left, right):
    return lax.dot_general(
        left, right, (((0,), (0,)), ((), ())), preferred_element_type=jnp.float32
    )


def kernel(
    subs,
    slabs,
    adjacency_hbm,
    piece_slot_hbm,
    tile_range_hbm,
    eigenvalues_hbm,
    modes,
    coupling_k,
    coupling_m,
    interface_k_hbm,
    interface_m_hbm,
    reduced_k,
    reduced_m,
    adjacency,
    piece_slot,
    tile_range,
    eigenvalues,
    interface_k,
    interface_m,
    tile_k,
    tile_m,
    outgoing,
    columns,
    all_modes,
    blocks,
    arrived,
    small_sem,
    local_sem,
    modes_send,
    modes_recv,
    columns_send,
    columns_recv,
    blocks_send,
    blocks_recv,
):
    sub = lax.axis_index("sub")
    slab = lax.axis_index("slab")
    group = subs // slabs
    adj = adjacency.shape[1]
    owned, quarter, width = interface_k.shape
    rows = modes.shape[1]
    home = sub // group

    loads = [
        pltpu.make_async_copy(
            whole.at[0, :, a * width : (a + 1) * width], tile.at[a], local_sem.at[kind, a]
        )
        for a in range(adj)
        for kind, (whole, tile) in enumerate(((coupling_k, tile_k), (coupling_m, tile_m)))
    ]
    routing = [
        pltpu.make_async_copy(whole, held, small_sem.at[n])
        for n, (whole, held) in enumerate((
            (adjacency_hbm, adjacency), (piece_slot_hbm, piece_slot), (tile_range_hbm, tile_range)
        ))
    ]
    late = [
        pltpu.make_async_copy(whole, held, small_sem.at[3 + n])
        for n, (whole, held) in enumerate((
            (eigenvalues_hbm, eigenvalues),
            (interface_k_hbm, interface_k),
            (interface_m_hbm, interface_m),
        ))
    ]
    loads = routing + loads + late
    loads.append(pltpu.make_async_copy(modes.at[0], all_modes.at[slab], modes_recv.at[slab]))
    for load in loads:
        load.start()

    barrier = pltpu.get_barrier_semaphore()
    for turn in range(1, slabs):
        pl.semaphore_signal(
            barrier, inc=1, device_id=(sub, lax.rem(slab + turn, slabs)), device_id_type=MESH
        )
    for turn in range(1, subs):
        pl.semaphore_signal(
            barrier, inc=1, device_id=(lax.rem(sub + turn, subs), home), device_id_type=MESH
        )

    @pl.when(home != slab)
    def _():
        pl.semaphore_signal(barrier, inc=1, device_id=(sub, home), device_id_type=MESH)

    for load in routing:
        load.wait()
    slots = [piece_slot[adjacency[sub, a]] for a in range(adj)]

    def owner_of(part, step):
        return part * group + lax.rem(step + sub + 1, group)

    for load in loads[len(routing) : -1 - len(late)]:
        load.wait()
    row_index = slab * rows + lax.broadcasted_iota(jnp.int32, (rows, width), 0)
    for turn in list(range(1, slabs)) + [0]:
        part = lax.rem(slab + turn, slabs)
        for step in range(group):
            owner = owner_of(part, step)
            place = jnp.int32(0)
            for a in range(adj):
                mine = (slots[a] >= owner * owned) & (slots[a] < (owner + 1) * owned)
                place = jnp.where(mine, jnp.int32(a), place)
            start = tile_range[0, 0, place]
            finish = tile_range[0, 1, place]
            live = ((row_index >= start) & (row_index < finish)).astype(jnp.float32)
            live = live.astype(jnp.bfloat16)
            stiff = tile_k[place] * live
            mass = tile_m[place] * live
            if turn == 0:
                columns[step, slab, :, 0:width] = stiff
                columns[step, slab, :, width:] = mass
            else:
                outgoing[step, turn - 1, :, 0:width] = stiff
                outgoing[step, turn - 1, :, width:] = mass

    @pl.when(home != slab)
    def _():
        pl.semaphore_wait(barrier, slabs - 1 + group * slabs)

    @pl.when(home == slab)
    def _():
        pl.semaphore_wait(barrier, slabs - 1 + group * slabs - 1)

    sends = []
    for turn in range(1, slabs):
        part = lax.rem(slab + turn, slabs)
        copy = pltpu.make_async_remote_copy(
            src_ref=modes.at[0],
            dst_ref=all_modes.at[slab],
            send_sem=modes_send.at[turn - 1],
            recv_sem=modes_recv.at[slab],
            device_id=(sub, part),
            device_id_type=MESH,
        )
        copy.start()
        sends.append(copy)
    for step in range(group):
        for turn in range(1, slabs):
            part = lax.rem(slab + turn, slabs)
            copy = pltpu.make_async_remote_copy(
                src_ref=outgoing.at[step, turn - 1],
                dst_ref=columns.at[step, slab],
                send_sem=columns_send.at[step, turn - 1],
                recv_sem=columns_recv.at[step, slab],
                device_id=(sub, part),
                device_id_type=MESH,
            )
            copy.start()
            sends.append(copy)

    takes = []
    for other in range(subs):
        theirs = [piece_slot[adjacency[other, a]] for a in range(adj)]
        takes.append([
            functools.reduce(
                lambda x, y: x | y,
                [(slot == sub * owned + q).astype(jnp.int32) for slot in theirs],
            )
            for q in range(owned)
        ])
    for load in late:
        load.wait()
    eig = jnp.broadcast_to(eigenvalues[...], (width, modes.shape[2])).T
    root = lax.rsqrt(eig)

    loads[-1].wait()
    for turn in range(1, slabs):
        part = lax.rem(slab + turn, slabs)
        pltpu.make_async_copy(all_modes.at[part], all_modes.at[part], modes_recv.at[part]).wait()
    basis = all_modes[...].reshape(slabs * rows, modes.shape[2])
    for step in range(group):
        for turn in range(1, slabs):
            part = lax.rem(slab + turn, slabs)
            pltpu.make_async_copy(
                columns.at[step, part], columns.at[step, part], columns_recv.at[step, part]
            ).wait()
        proj = contract_rows(basis, columns[step].reshape(slabs * rows, 2 * width))
        proj_s, proj_v = proj[:, :width], proj[:, width:]
        first = (proj_s * root).astype(jnp.bfloat16)
        second = (proj_s / eig - proj_v).astype(jnp.bfloat16)
        third = proj_v.astype(jnp.bfloat16)
        gram_k = contract_rows(first, first)
        gram_m = contract_rows(
            jnp.concatenate([second, third]), jnp.concatenate([second, -third])
        )
        blocks[step, :, 0] = gram_k.astype(jnp.bfloat16).reshape(slabs, quarter, width)
        blocks[step, :, 1] = gram_m.astype(jnp.bfloat16).reshape(slabs, quarter, width)
        owner = owner_of(slab, step)
        for turn in range(1, slabs + 1):
            part = lax.rem(slab + turn, slabs)
            copy = pltpu.make_async_remote_copy(
                src_ref=blocks.at[step, part],
                dst_ref=arrived.at[sub],
                send_sem=blocks_send.at[step, turn - 1],
                recv_sem=blocks_recv.at[sub],
                device_id=(owner, part),
                device_id_type=MESH,
            )
            if turn < slabs:
                copy.start()
                sends.append(copy)
            else:
                pl.when(owner != sub)(copy.start)

                @pl.when(owner == sub)
                def _():
                    arrived[sub] = blocks[step, slab]

    total = [[interface_k[q] for q in range(owned)], [interface_m[q] for q in range(owned)]]
    for other in range(subs):

        @pl.when((other != sub) | (home != slab))
        def _():
            pltpu.make_async_copy(
                arrived.at[other], arrived.at[other], blocks_recv.at[other]
            ).wait()

        for kind in range(2):
            term = arrived[other, kind].astype(jnp.float32)
            for q in range(owned):
                total[kind][q] = total[kind][q] + jnp.where(takes[other][q] > 0, term, 0.0)
    for q in range(owned):
        reduced_k[q] = total[0][q]
        reduced_m[q] = total[1][q]

    for copy in sends:
        copy.wait_send()
    for step in range(group):

        @pl.when(owner_of(slab, step) != sub)
        def _():
            pltpu.make_async_copy(
                blocks.at[step, slab], blocks.at[step, slab], blocks_send.at[step, slabs - 1]
            ).wait()


def dense_body(
    subs,
    slabs,
    mode_shapes,
    coupling_k,
    coupling_m,
    tile_range,
    eigenvalues,
    adjacency,
    piece_slot,
    interface_k,
    interface_m,
):
    _, rows, mode_count = mode_shapes.shape
    adj = adjacency.shape[1]
    owned, quarter, width = interface_k.shape
    group = subs // slabs
    vmem = pl.BlockSpec(memory_space=pltpu.VMEM)
    hbm = pl.BlockSpec(memory_space=pltpu.HBM)
    out = jax.ShapeDtypeStruct(interface_k.shape, interface_k.dtype)
    return pl.pallas_call(
        functools.partial(kernel, subs, slabs),
        out_shape=(out, out),
        in_specs=[hbm] * 9,
        out_specs=(vmem, vmem),
        scratch_shapes=[
            pltpu.SMEM(adjacency.shape, adjacency.dtype),
            pltpu.SMEM(piece_slot.shape, piece_slot.dtype),
            pltpu.SMEM(tile_range.shape, tile_range.dtype),
            pltpu.VMEM(eigenvalues.shape, eigenvalues.dtype),
            pltpu.VMEM(interface_k.shape, interface_k.dtype),
            pltpu.VMEM(interface_m.shape, interface_m.dtype),
            pltpu.VMEM((adj, rows, width), jnp.bfloat16),
            pltpu.VMEM((adj, rows, width), jnp.bfloat16),
            pltpu.VMEM((group, slabs - 1, rows, 2 * width), jnp.bfloat16),
            pltpu.VMEM((group, slabs, rows, 2 * width), jnp.bfloat16),
            pltpu.VMEM((slabs, rows, mode_count), jnp.bfloat16),
            pltpu.VMEM((group, slabs, 2, quarter, width), jnp.bfloat16),
            pltpu.VMEM((subs, 2, quarter, width), jnp.bfloat16),
            pltpu.SemaphoreType.DMA((6,)),
            pltpu.SemaphoreType.DMA((2, adj)),
            pltpu.SemaphoreType.DMA((slabs - 1,)),
            pltpu.SemaphoreType.DMA((slabs,)),
            pltpu.SemaphoreType.DMA((group, slabs - 1)),
            pltpu.SemaphoreType.DMA((group, slabs)),
            pltpu.SemaphoreType.DMA((group, slabs)),
            pltpu.SemaphoreType.DMA((subs,)),
        ],
        compiler_params=pltpu.CompilerParams(
            collective_id=0, has_side_effects=True, vmem_limit_bytes=64 * 1024 * 1024
        ),
    )(
        adjacency,
        piece_slot,
        tile_range,
        eigenvalues,
        mode_shapes,
        coupling_k,
        coupling_m,
        interface_k,
        interface_m,
    )


def sparse_body(
    mode_shapes,
    coupling_k,
    coupling_m,
    tile_range,
    eigenvalues,
    adjacency,
    piece_slot,
    interface_k,
    interface_m,
):
    row_count = mode_shapes.shape[1]
    mode_count = mode_shapes.shape[2]
    adj_count = adjacency.shape[1]
    piece_width = interface_k.shape[2]
    owned_count = interface_k.shape[0]
    quarter_rows = interface_k.shape[1]
    sub_count = lax.axis_size("sub")
    slab_pos = lax.axis_index("slab")
    sub_pos = lax.axis_index("sub")
    row_index = slab_pos * row_count + lax.iota(jnp.int32, row_count)
    live = (
        (row_index[:, None] >= tile_range[0, 0][None, :])
        & (row_index[:, None] < tile_range[0, 1][None, :])
    ).astype(jnp.bfloat16)
    stiff_rows = (
        coupling_k[0].reshape(row_count, adj_count, piece_width) * live[:, :, None]
    ).reshape(row_count, adj_count * piece_width)
    mass_rows = (
        coupling_m[0].reshape(row_count, adj_count, piece_width) * live[:, :, None]
    ).reshape(row_count, adj_count * piece_width)
    part_s = jnp.einsum("rm,rc->mc", mode_shapes[0], stiff_rows, preferred_element_type=jnp.float32)
    part_v = jnp.einsum("rm,rc->mc", mode_shapes[0], mass_rows, preferred_element_type=jnp.float32)
    proj_s, proj_v = lax.psum((part_s, part_v), "slab")
    eig_held = eigenvalues[0]
    eig_col = eig_held[:, None]
    first = (proj_s * lax.rsqrt(eig_col)).astype(jnp.bfloat16)
    second = (proj_s / eig_col - proj_v).astype(jnp.bfloat16)
    third = proj_v.astype(jnp.bfloat16)
    stacked = jnp.stack([first, second, third]).reshape(3, mode_count, adj_count, piece_width)
    my_slots = piece_slot[adjacency[sub_pos]]
    owner_hot = (
        my_slots[None, :] // owned_count == lax.iota(jnp.int32, sub_count)[:, None]
    ).astype(jnp.bfloat16)
    outgoing = jnp.einsum(
        "oa,kmab->okmb", owner_hot, stacked, preferred_element_type=jnp.float32
    ).astype(jnp.bfloat16)
    incoming = lax.all_to_all(outgoing, "sub", split_axis=0, concat_axis=0, tiled=True)
    all_slots = piece_slot[adjacency]
    targets = sub_pos * owned_count + lax.iota(jnp.int32, owned_count)
    select = jnp.any(all_slots[:, :, None] == targets[None, None, :], axis=1).astype(jnp.bfloat16)

    def piece_gram(weights):
        picked = incoming * weights[:, None, None, None]
        left_side = lax.dynamic_slice_in_dim(picked, slab_pos * quarter_rows, quarter_rows, 3)
        gram_stiff = jnp.einsum(
            "smb,smc->bc", left_side[:, 0], incoming[:, 0], preferred_element_type=jnp.float32
        )
        gram_mass = jnp.einsum(
            "smb,smc->bc", left_side[:, 1], incoming[:, 1], preferred_element_type=jnp.float32
        )
        gram_mass = gram_mass - jnp.einsum(
            "smb,smc->bc", left_side[:, 2], incoming[:, 2], preferred_element_type=jnp.float32
        )
        return (gram_stiff, gram_mass)

    gram_k, gram_m = lax.map(piece_gram, select.T)
    return (interface_k + gram_k, interface_m + gram_m)


def body(subs, slabs, *arrays):
    adjacency = arrays[5]
    if adjacency.shape[1] == subs and subs % slabs == 0:
        return dense_body(subs, slabs, *arrays)
    return sparse_body(*arrays)


def solution(mesh):
    placed = (
        P("sub", "slab", None),
        P("sub", "slab", None),
        P("sub", "slab", None),
        P("sub", None, None),
        P("sub", None),
        P(),
        P(),
        P("sub", "slab", None),
        P("sub", "slab", None),
    )
    return jax.shard_map(
        functools.partial(body, mesh.shape["sub"], mesh.shape["slab"]),
        mesh=mesh,
        in_specs=placed,
        out_specs=(P("sub", "slab", None), P("sub", "slab", None)),
        check_vma=False,
    )
```

```python
import functools

import jax
import jax.numpy as jnp
from jax import lax
from jax.experimental import pallas as pl
from jax.experimental.pallas import tpu as pltpu
from jax.sharding import PartitionSpec as P

MESH = pl.DeviceIdType.MESH


def contract_rows(left, right):
    return lax.dot_general(
        left, right, (((0,), (0,)), ((), ())), preferred_element_type=jnp.float32
    )


def kernel(
    subs,
    slabs,
    adjacency_hbm,
    piece_slot_hbm,
    tile_range_hbm,
    eigenvalues_hbm,
    modes,
    coupling_k,
    coupling_m,
    gram,
    adjacency,
    piece_slot,
    tile_range,
    eigenvalues,
    tile_k,
    tile_m,
    outgoing,
    columns,
    all_modes,
    blocks,
    arrived,
    small_sem,
    local_sem,
    modes_send,
    modes_recv,
    columns_send,
    columns_recv,
    blocks_send,
    blocks_recv,
):
    sub = lax.axis_index("sub")
    slab = lax.axis_index("slab")
    group = subs // slabs
    adj = adjacency.shape[1]
    _, owned, quarter, width = gram.shape
    rows = modes.shape[1]
    home = sub // group

    loads = [
        pltpu.make_async_copy(
            whole.at[0, :, a * width : (a + 1) * width], tile.at[a], local_sem.at[kind, a]
        )
        for a in range(adj)
        for kind, (whole, tile) in enumerate(((coupling_k, tile_k), (coupling_m, tile_m)))
    ]
    routing = [
        pltpu.make_async_copy(whole, held, small_sem.at[n])
        for n, (whole, held) in enumerate((
            (adjacency_hbm, adjacency), (piece_slot_hbm, piece_slot), (tile_range_hbm, tile_range)
        ))
    ]
    late = [
        pltpu.make_async_copy(whole, held, small_sem.at[3 + n])
        for n, (whole, held) in enumerate(((eigenvalues_hbm, eigenvalues),))
    ]
    loads = routing + loads + late
    loads.append(pltpu.make_async_copy(modes.at[0], all_modes.at[slab], modes_recv.at[slab]))
    for load in loads:
        load.start()

    barrier = pltpu.get_barrier_semaphore()
    for turn in range(1, slabs):
        pl.semaphore_signal(
            barrier, inc=1, device_id=(sub, lax.rem(slab + turn, slabs)), device_id_type=MESH
        )
    for turn in range(1, subs):
        pl.semaphore_signal(
            barrier, inc=1, device_id=(lax.rem(sub + turn, subs), home), device_id_type=MESH
        )

    @pl.when(home != slab)
    def _():
        pl.semaphore_signal(barrier, inc=1, device_id=(sub, home), device_id_type=MESH)

    for load in routing:
        load.wait()
    slots = [piece_slot[adjacency[sub, a]] for a in range(adj)]

    def owner_of(part, step):
        return part * group + lax.rem(step + sub + 1, group)

    for load in loads[len(routing) : -1 - len(late)]:
        load.wait()
    row_index = slab * rows + lax.broadcasted_iota(jnp.int32, (rows, width), 0)
    for turn in list(range(1, slabs)) + [0]:
        part = lax.rem(slab + turn, slabs)
        for step in range(group):
            owner = owner_of(part, step)
            place = jnp.int32(0)
            for a in range(adj):
                mine = (slots[a] >= owner * owned) & (slots[a] < (owner + 1) * owned)
                place = jnp.where(mine, jnp.int32(a), place)
            start = tile_range[0, 0, place]
            finish = tile_range[0, 1, place]
            live = ((row_index >= start) & (row_index < finish)).astype(jnp.float32)
            live = live.astype(jnp.bfloat16)
            stiff = tile_k[place] * live
            mass = tile_m[place] * live
            if turn == 0:
                columns[step, slab, :, 0:width] = stiff
                columns[step, slab, :, width:] = mass
            else:
                outgoing[step, turn - 1, :, 0:width] = stiff
                outgoing[step, turn - 1, :, width:] = mass

    @pl.when(home != slab)
    def _():
        pl.semaphore_wait(barrier, slabs - 1 + group * slabs)

    @pl.when(home == slab)
    def _():
        pl.semaphore_wait(barrier, slabs - 1 + group * slabs - 1)

    sends = []
    for turn in range(1, slabs):
        part = lax.rem(slab + turn, slabs)
        copy = pltpu.make_async_remote_copy(
            src_ref=modes.at[0],
            dst_ref=all_modes.at[slab],
            send_sem=modes_send.at[turn - 1],
            recv_sem=modes_recv.at[slab],
            device_id=(sub, part),
            device_id_type=MESH,
        )
        copy.start()
        sends.append(copy)
    for step in range(group):
        for turn in range(1, slabs):
            part = lax.rem(slab + turn, slabs)
            copy = pltpu.make_async_remote_copy(
                src_ref=outgoing.at[step, turn - 1],
                dst_ref=columns.at[step, slab],
                send_sem=columns_send.at[step, turn - 1],
                recv_sem=columns_recv.at[step, slab],
                device_id=(sub, part),
                device_id_type=MESH,
            )
            copy.start()
            sends.append(copy)

    takes = []
    for other in range(subs):
        theirs = [piece_slot[adjacency[other, a]] for a in range(adj)]
        takes.append([
            functools.reduce(
                lambda x, y: x | y,
                [(slot == sub * owned + q).astype(jnp.int32) for slot in theirs],
            )
            for q in range(owned)
        ])
    for load in late:
        load.wait()
    eig = jnp.broadcast_to(eigenvalues[...], (width, modes.shape[2])).T
    root = lax.rsqrt(eig)

    loads[-1].wait()
    for turn in range(1, slabs):
        part = lax.rem(slab + turn, slabs)
        pltpu.make_async_copy(all_modes.at[part], all_modes.at[part], modes_recv.at[part]).wait()
    basis = all_modes[...].reshape(slabs * rows, modes.shape[2])
    for step in range(group):
        for turn in range(1, slabs):
            part = lax.rem(slab + turn, slabs)
            pltpu.make_async_copy(
                columns.at[step, part], columns.at[step, part], columns_recv.at[step, part]
            ).wait()
        proj = contract_rows(basis, columns[step].reshape(slabs * rows, 2 * width))
        proj_s, proj_v = proj[:, :width], proj[:, width:]
        first = (proj_s * root).astype(jnp.bfloat16)
        second = (proj_s / eig - proj_v).astype(jnp.bfloat16)
        third = proj_v.astype(jnp.bfloat16)
        gram_k = contract_rows(first, first)
        gram_m = contract_rows(
            jnp.concatenate([second, third]), jnp.concatenate([second, -third])
        )
        blocks[step, :, 0] = gram_k.astype(jnp.bfloat16).reshape(slabs, quarter, width)
        blocks[step, :, 1] = gram_m.astype(jnp.bfloat16).reshape(slabs, quarter, width)
        owner = owner_of(slab, step)
        for turn in range(1, slabs + 1):
            part = lax.rem(slab + turn, slabs)
            copy = pltpu.make_async_remote_copy(
                src_ref=blocks.at[step, part],
                dst_ref=arrived.at[sub],
                send_sem=blocks_send.at[step, turn - 1],
                recv_sem=blocks_recv.at[sub],
                device_id=(owner, part),
                device_id_type=MESH,
            )
            if turn < slabs:
                copy.start()
                sends.append(copy)
            else:
                pl.when(owner != sub)(copy.start)

                @pl.when(owner == sub)
                def _():
                    arrived[sub] = blocks[step, slab]

    total = [[jnp.zeros((quarter, width), jnp.float32)] * owned for _ in range(2)]
    for other in range(subs):

        @pl.when((other != sub) | (home != slab))
        def _():
            pltpu.make_async_copy(
                arrived.at[other], arrived.at[other], blocks_recv.at[other]
            ).wait()

        for kind in range(2):
            term = arrived[other, kind].astype(jnp.float32)
            for q in range(owned):
                total[kind][q] = total[kind][q] + jnp.where(takes[other][q] > 0, term, 0.0)
    for q in range(owned):
        gram[0, q] = total[0][q]
        gram[1, q] = total[1][q]

    for copy in sends:
        copy.wait_send()
    for step in range(group):

        @pl.when(owner_of(slab, step) != sub)
        def _():
            pltpu.make_async_copy(
                blocks.at[step, slab], blocks.at[step, slab], blocks_send.at[step, slabs - 1]
            ).wait()


def dense_body(
    subs,
    slabs,
    mode_shapes,
    coupling_k,
    coupling_m,
    tile_range,
    eigenvalues,
    adjacency,
    piece_slot,
    interface_k,
    interface_m,
):
    _, rows, mode_count = mode_shapes.shape
    adj = adjacency.shape[1]
    owned, quarter, width = interface_k.shape
    group = subs // slabs
    vmem = pl.BlockSpec(memory_space=pltpu.VMEM)
    hbm = pl.BlockSpec(memory_space=pltpu.HBM)
    gram = pl.pallas_call(
        functools.partial(kernel, subs, slabs),
        out_shape=jax.ShapeDtypeStruct((2,) + interface_k.shape, jnp.float32),
        in_specs=[hbm] * 7,
        out_specs=vmem,
        scratch_shapes=[
            pltpu.SMEM(adjacency.shape, adjacency.dtype),
            pltpu.SMEM(piece_slot.shape, piece_slot.dtype),
            pltpu.SMEM(tile_range.shape, tile_range.dtype),
            pltpu.VMEM(eigenvalues.shape, eigenvalues.dtype),
            pltpu.VMEM((adj, rows, width), jnp.bfloat16),
            pltpu.VMEM((adj, rows, width), jnp.bfloat16),
            pltpu.VMEM((group, slabs - 1, rows, 2 * width), jnp.bfloat16),
            pltpu.VMEM((group, slabs, rows, 2 * width), jnp.bfloat16),
            pltpu.VMEM((slabs, rows, mode_count), jnp.bfloat16),
            pltpu.VMEM((group, slabs, 2, quarter, width), jnp.bfloat16),
            pltpu.VMEM((subs, 2, quarter, width), jnp.bfloat16),
            pltpu.SemaphoreType.DMA((4,)),
            pltpu.SemaphoreType.DMA((2, adj)),
            pltpu.SemaphoreType.DMA((slabs - 1,)),
            pltpu.SemaphoreType.DMA((slabs,)),
            pltpu.SemaphoreType.DMA((group, slabs - 1)),
            pltpu.SemaphoreType.DMA((group, slabs)),
            pltpu.SemaphoreType.DMA((group, slabs)),
            pltpu.SemaphoreType.DMA((subs,)),
        ],
        compiler_params=pltpu.CompilerParams(
            collective_id=0, has_side_effects=True, vmem_limit_bytes=64 * 1024 * 1024
        ),
    )(
        adjacency,
        piece_slot,
        tile_range,
        eigenvalues,
        mode_shapes,
        coupling_k,
        coupling_m,
    )
    return (interface_k + gram[0], interface_m + gram[1])


def sparse_body(
    mode_shapes,
    coupling_k,
    coupling_m,
    tile_range,
    eigenvalues,
    adjacency,
    piece_slot,
    interface_k,
    interface_m,
):
    row_count = mode_shapes.shape[1]
    mode_count = mode_shapes.shape[2]
    adj_count = adjacency.shape[1]
    piece_width = interface_k.shape[2]
    owned_count = interface_k.shape[0]
    quarter_rows = interface_k.shape[1]
    sub_count = lax.axis_size("sub")
    slab_pos = lax.axis_index("slab")
    sub_pos = lax.axis_index("sub")
    row_index = slab_pos * row_count + lax.iota(jnp.int32, row_count)
    live = (
        (row_index[:, None] >= tile_range[0, 0][None, :])
        & (row_index[:, None] < tile_range[0, 1][None, :])
    ).astype(jnp.bfloat16)
    stiff_rows = (
        coupling_k[0].reshape(row_count, adj_count, piece_width) * live[:, :, None]
    ).reshape(row_count, adj_count * piece_width)
    mass_rows = (
        coupling_m[0].reshape(row_count, adj_count, piece_width) * live[:, :, None]
    ).reshape(row_count, adj_count * piece_width)
    part_s = jnp.einsum("rm,rc->mc", mode_shapes[0], stiff_rows, preferred_element_type=jnp.float32)
    part_v = jnp.einsum("rm,rc->mc", mode_shapes[0], mass_rows, preferred_element_type=jnp.float32)
    proj_s, proj_v = lax.psum((part_s, part_v), "slab")
    eig_held = eigenvalues[0]
    eig_col = eig_held[:, None]
    first = (proj_s * lax.rsqrt(eig_col)).astype(jnp.bfloat16)
    second = (proj_s / eig_col - proj_v).astype(jnp.bfloat16)
    third = proj_v.astype(jnp.bfloat16)
    stacked = jnp.stack([first, second, third]).reshape(3, mode_count, adj_count, piece_width)
    my_slots = piece_slot[adjacency[sub_pos]]
    owner_hot = (
        my_slots[None, :] // owned_count == lax.iota(jnp.int32, sub_count)[:, None]
    ).astype(jnp.bfloat16)
    outgoing = jnp.einsum(
        "oa,kmab->okmb", owner_hot, stacked, preferred_element_type=jnp.float32
    ).astype(jnp.bfloat16)
    incoming = lax.all_to_all(outgoing, "sub", split_axis=0, concat_axis=0, tiled=True)
    all_slots = piece_slot[adjacency]
    targets = sub_pos * owned_count + lax.iota(jnp.int32, owned_count)
    select = jnp.any(all_slots[:, :, None] == targets[None, None, :], axis=1).astype(jnp.bfloat16)

    def piece_gram(weights):
        picked = incoming * weights[:, None, None, None]
        left_side = lax.dynamic_slice_in_dim(picked, slab_pos * quarter_rows, quarter_rows, 3)
        gram_stiff = jnp.einsum(
            "smb,smc->bc", left_side[:, 0], incoming[:, 0], preferred_element_type=jnp.float32
        )
        gram_mass = jnp.einsum(
            "smb,smc->bc", left_side[:, 1], incoming[:, 1], preferred_element_type=jnp.float32
        )
        gram_mass = gram_mass - jnp.einsum(
            "smb,smc->bc", left_side[:, 2], incoming[:, 2], preferred_element_type=jnp.float32
        )
        return (gram_stiff, gram_mass)

    gram_k, gram_m = lax.map(piece_gram, select.T)
    return (interface_k + gram_k, interface_m + gram_m)


def body(subs, slabs, *arrays):
    adjacency = arrays[5]
    if adjacency.shape[1] == subs and subs % slabs == 0:
        return dense_body(subs, slabs, *arrays)
    return sparse_body(*arrays)


def solution(mesh):
    placed = (
        P("sub", "slab", None),
        P("sub", "slab", None),
        P("sub", "slab", None),
        P("sub", None, None),
        P("sub", None),
        P(),
        P(),
        P("sub", "slab", None),
        P("sub", "slab", None),
    )
    return jax.shard_map(
        functools.partial(body, mesh.shape["sub"], mesh.shape["slab"]),
        mesh=mesh,
        in_specs=placed,
        out_specs=(P("sub", "slab", None), P("sub", "slab", None)),
        check_vma=False,
    )
```

```python
import functools

import jax
import jax.numpy as jnp
from jax import lax
from jax.experimental import pallas as pl
from jax.experimental.pallas import tpu as pltpu
from jax.sharding import PartitionSpec as P

MESH = pl.DeviceIdType.MESH


def contract_rows(left, right):
    return lax.dot_general(
        left, right, (((0,), (0,)), ((), ())), preferred_element_type=jnp.float32
    )


def kernel(
    subs,
    slabs,
    adjacency_hbm,
    piece_slot_hbm,
    tile_range_hbm,
    eigenvalues_hbm,
    modes,
    coupling_k,
    coupling_m,
    gram,
    adjacency,
    piece_slot,
    tile_range,
    eigenvalues,
    my_modes,
    tile_k,
    tile_m,
    outgoing,
    columns,
    all_modes,
    blocks,
    arrived,
    small_sem,
    local_sem,
    modes_send,
    modes_recv,
    columns_send,
    columns_recv,
    blocks_send,
    blocks_recv,
):
    sub = lax.axis_index("sub")
    slab = lax.axis_index("slab")
    group = subs // slabs
    adj = adjacency.shape[1]
    _, owned, quarter, width = gram.shape
    rows = modes.shape[1]
    home = sub // group

    loads = [
        pltpu.make_async_copy(
            whole.at[0, :, a * width : (a + 1) * width], tile.at[a], local_sem.at[kind, a]
        )
        for a in range(adj)
        for kind, (whole, tile) in enumerate(((coupling_k, tile_k), (coupling_m, tile_m)))
    ]
    routing = [
        pltpu.make_async_copy(whole, held, small_sem.at[n])
        for n, (whole, held) in enumerate((
            (adjacency_hbm, adjacency), (piece_slot_hbm, piece_slot), (tile_range_hbm, tile_range)
        ))
    ]
    late = [
        pltpu.make_async_copy(whole, held, small_sem.at[3 + n])
        for n, (whole, held) in enumerate(((eigenvalues_hbm, eigenvalues),))
    ]
    late.append(pltpu.make_async_copy(modes.at[0], my_modes, small_sem.at[4]))
    for load in routing + late[1:] + loads:
        load.start()

    barrier = pltpu.get_barrier_semaphore()
    for turn in range(1, slabs):
        pl.semaphore_signal(
            barrier, inc=1, device_id=(sub, lax.rem(slab + turn, slabs)), device_id_type=MESH
        )
    for turn in range(1, subs):
        pl.semaphore_signal(
            barrier, inc=1, device_id=(lax.rem(sub + turn, subs), home), device_id_type=MESH
        )

    @pl.when(home != slab)
    def _():
        pl.semaphore_signal(barrier, inc=1, device_id=(sub, home), device_id_type=MESH)

    late[0].start()
    late[1].wait()
    half = rows // 2
    all_modes[slab] = jnp.concatenate([my_modes[:half], my_modes[half:]], axis=1)
    for load in routing:
        load.wait()
    slots = [piece_slot[adjacency[sub, a]] for a in range(adj)]

    def owner_of(part, step):
        return part * group + lax.rem(step + sub + 1, group)

    plan = []
    for step in range(group):
        for turn in list(range(1, slabs)) + [0]:
            owner = owner_of(lax.rem(slab + turn, slabs), step)
            place = jnp.int32(0)
            for a in range(adj):
                mine = (slots[a] >= owner * owned) & (slots[a] < (owner + 1) * owned)
                place = jnp.where(mine, jnp.int32(a), place)
            start = tile_range[0, 0, place] - slab * rows
            finish = tile_range[0, 1, place] - slab * rows
            plan.append((step, turn, place, start, finish))
    row_index = lax.broadcasted_iota(jnp.int32, (rows, width), 0)
    for load in loads:
        load.wait()
    for step, turn, place, start, finish in plan:
        live = ((row_index >= start) & (row_index < finish)).astype(jnp.float32)
        live = live.astype(jnp.bfloat16)
        stiff = tile_k[place] * live
        mass = tile_m[place] * live
        if turn == 0:
            columns[step, slab, :, 0:width] = stiff
            columns[step, slab, :, width:] = mass
        else:
            outgoing[step, turn - 1, :, 0:width] = stiff
            outgoing[step, turn - 1, :, width:] = mass

    @pl.when(home != slab)
    def _():
        pl.semaphore_wait(barrier, slabs - 1 + group * slabs)

    @pl.when(home == slab)
    def _():
        pl.semaphore_wait(barrier, slabs - 1 + group * slabs - 1)

    sends = []
    for turn in range(1, slabs):
        part = lax.rem(slab + turn, slabs)
        copy = pltpu.make_async_remote_copy(
            src_ref=all_modes.at[slab],
            dst_ref=all_modes.at[slab],
            send_sem=modes_send.at[turn - 1],
            recv_sem=modes_recv.at[slab],
            device_id=(sub, part),
            device_id_type=MESH,
        )
        copy.start()
        sends.append(copy)
    for step in range(group):
        for turn in range(1, slabs):
            part = lax.rem(slab + turn, slabs)
            copy = pltpu.make_async_remote_copy(
                src_ref=outgoing.at[step, turn - 1],
                dst_ref=columns.at[step, slab],
                send_sem=columns_send.at[step, turn - 1],
                recv_sem=columns_recv.at[step, slab],
                device_id=(sub, part),
                device_id_type=MESH,
            )
            copy.start()
            sends.append(copy)

    takes = []
    for other in range(subs):
        theirs = [piece_slot[adjacency[other, a]] for a in range(adj)]
        takes.append([
            functools.reduce(
                lambda x, y: x | y,
                [(slot == sub * owned + q).astype(jnp.int32) for slot in theirs],
            )
            for q in range(owned)
        ])
    late[0].wait()
    eig = jnp.broadcast_to(eigenvalues[...], (width, modes.shape[2])).T
    root = lax.rsqrt(eig)

    for turn in range(1, slabs):
        part = lax.rem(slab + turn, slabs)
        pltpu.make_async_copy(all_modes.at[part], all_modes.at[part], modes_recv.at[part]).wait()
    mode_count = modes.shape[2]
    basis = jnp.concatenate([
        all_modes[part, :, side * mode_count : (side + 1) * mode_count]
        for part in range(slabs)
        for side in range(2)
    ]).T
    for step in range(group):
        for turn in range(1, slabs):
            part = lax.rem(slab + turn, slabs)
            pltpu.make_async_copy(
                columns.at[step, part], columns.at[step, part], columns_recv.at[step, part]
            ).wait()
        proj = jnp.dot(
            basis,
            columns[step].reshape(slabs * rows, 2 * width),
            preferred_element_type=jnp.float32,
        )
        proj_s, proj_v = proj[:, :width], proj[:, width:]
        first = (proj_s * root).astype(jnp.bfloat16)
        second = (proj_s / eig - proj_v).astype(jnp.bfloat16)
        third = proj_v.astype(jnp.bfloat16)
        gram_k = contract_rows(first, first)
        gram_m = contract_rows(
            jnp.concatenate([second, third]), jnp.concatenate([second, -third])
        )
        blocks[step, :, 0] = gram_k.astype(jnp.bfloat16).reshape(slabs, quarter, width)
        blocks[step, :, 1] = gram_m.astype(jnp.bfloat16).reshape(slabs, quarter, width)
        owner = owner_of(slab, step)
        for turn in range(1, slabs + 1):
            part = lax.rem(slab + turn, slabs)
            copy = pltpu.make_async_remote_copy(
                src_ref=blocks.at[step, part],
                dst_ref=arrived.at[sub],
                send_sem=blocks_send.at[step, turn - 1],
                recv_sem=blocks_recv.at[sub],
                device_id=(owner, part),
                device_id_type=MESH,
            )
            if turn < slabs:
                copy.start()
                sends.append(copy)
            else:
                pl.when(owner != sub)(copy.start)

                @pl.when(owner == sub)
                def _():
                    arrived[sub] = blocks[step, slab]

    for copy in sends:
        copy.wait_send()
    for step in range(group):

        @pl.when(owner_of(slab, step) != sub)
        def _():
            pltpu.make_async_copy(
                blocks.at[step, slab], blocks.at[step, slab], blocks_send.at[step, slabs - 1]
            ).wait()

    total = [[jnp.zeros((quarter, width), jnp.float32)] * owned for _ in range(2)]
    for other in range(subs):

        @pl.when((other != sub) | (home != slab))
        def _():
            pltpu.make_async_copy(
                arrived.at[other], arrived.at[other], blocks_recv.at[other]
            ).wait()

        for kind in range(2):
            term = arrived[other, kind].astype(jnp.float32)
            for q in range(owned):
                total[kind][q] = total[kind][q] + jnp.where(takes[other][q] > 0, term, 0.0)
    for q in range(owned):
        gram[0, q] = total[0][q]
        gram[1, q] = total[1][q]


def dense_body(
    subs,
    slabs,
    mode_shapes,
    coupling_k,
    coupling_m,
    tile_range,
    eigenvalues,
    adjacency,
    piece_slot,
    interface_k,
    interface_m,
):
    _, rows, mode_count = mode_shapes.shape
    adj = adjacency.shape[1]
    owned, quarter, width = interface_k.shape
    group = subs // slabs
    vmem = pl.BlockSpec(memory_space=pltpu.VMEM)
    hbm = pl.BlockSpec(memory_space=pltpu.HBM)
    gram = pl.pallas_call(
        functools.partial(kernel, subs, slabs),
        out_shape=jax.ShapeDtypeStruct((2,) + interface_k.shape, jnp.float32),
        in_specs=[hbm] * 7,
        out_specs=vmem,
        scratch_shapes=[
            pltpu.SMEM(adjacency.shape, adjacency.dtype),
            pltpu.SMEM(piece_slot.shape, piece_slot.dtype),
            pltpu.SMEM(tile_range.shape, tile_range.dtype),
            pltpu.VMEM(eigenvalues.shape, eigenvalues.dtype),
            pltpu.VMEM((rows, mode_count), jnp.bfloat16),
            pltpu.VMEM((adj, rows, width), jnp.bfloat16),
            pltpu.VMEM((adj, rows, width), jnp.bfloat16),
            pltpu.VMEM((group, slabs - 1, rows, 2 * width), jnp.bfloat16),
            pltpu.VMEM((group, slabs, rows, 2 * width), jnp.bfloat16),
            pltpu.VMEM((slabs, rows // 2, 2 * mode_count), jnp.bfloat16),
            pltpu.VMEM((group, slabs, 2, quarter, width), jnp.bfloat16),
            pltpu.VMEM((subs, 2, quarter, width), jnp.bfloat16),
            pltpu.SemaphoreType.DMA((5,)),
            pltpu.SemaphoreType.DMA((2, adj)),
            pltpu.SemaphoreType.DMA((slabs - 1,)),
            pltpu.SemaphoreType.DMA((slabs,)),
            pltpu.SemaphoreType.DMA((group, slabs - 1)),
            pltpu.SemaphoreType.DMA((group, slabs)),
            pltpu.SemaphoreType.DMA((group, slabs)),
            pltpu.SemaphoreType.DMA((subs,)),
        ],
        compiler_params=pltpu.CompilerParams(
            collective_id=0, has_side_effects=True, vmem_limit_bytes=56 * 1024 * 1024
        ),
    )(
        adjacency,
        piece_slot,
        tile_range,
        eigenvalues,
        mode_shapes,
        coupling_k,
        coupling_m,
    )
    return (interface_k + gram[0], interface_m + gram[1])


def sparse_body(
    mode_shapes,
    coupling_k,
    coupling_m,
    tile_range,
    eigenvalues,
    adjacency,
    piece_slot,
    interface_k,
    interface_m,
):
    row_count = mode_shapes.shape[1]
    mode_count = mode_shapes.shape[2]
    adj_count = adjacency.shape[1]
    piece_width = interface_k.shape[2]
    owned_count = interface_k.shape[0]
    quarter_rows = interface_k.shape[1]
    sub_count = lax.axis_size("sub")
    slab_pos = lax.axis_index("slab")
    sub_pos = lax.axis_index("sub")
    row_index = slab_pos * row_count + lax.iota(jnp.int32, row_count)
    live = (
        (row_index[:, None] >= tile_range[0, 0][None, :])
        & (row_index[:, None] < tile_range[0, 1][None, :])
    ).astype(jnp.bfloat16)
    stiff_rows = (
        coupling_k[0].reshape(row_count, adj_count, piece_width) * live[:, :, None]
    ).reshape(row_count, adj_count * piece_width)
    mass_rows = (
        coupling_m[0].reshape(row_count, adj_count, piece_width) * live[:, :, None]
    ).reshape(row_count, adj_count * piece_width)
    part_s = jnp.einsum("rm,rc->mc", mode_shapes[0], stiff_rows, preferred_element_type=jnp.float32)
    part_v = jnp.einsum("rm,rc->mc", mode_shapes[0], mass_rows, preferred_element_type=jnp.float32)
    proj_s, proj_v = lax.psum((part_s, part_v), "slab")
    eig_held = eigenvalues[0]
    eig_col = eig_held[:, None]
    first = (proj_s * lax.rsqrt(eig_col)).astype(jnp.bfloat16)
    second = (proj_s / eig_col - proj_v).astype(jnp.bfloat16)
    third = proj_v.astype(jnp.bfloat16)
    stacked = jnp.stack([first, second, third]).reshape(3, mode_count, adj_count, piece_width)
    my_slots = piece_slot[adjacency[sub_pos]]
    owner_hot = (
        my_slots[None, :] // owned_count == lax.iota(jnp.int32, sub_count)[:, None]
    ).astype(jnp.bfloat16)
    outgoing = jnp.einsum(
        "oa,kmab->okmb", owner_hot, stacked, preferred_element_type=jnp.float32
    ).astype(jnp.bfloat16)
    incoming = lax.all_to_all(outgoing, "sub", split_axis=0, concat_axis=0, tiled=True)
    all_slots = piece_slot[adjacency]
    targets = sub_pos * owned_count + lax.iota(jnp.int32, owned_count)
    select = jnp.any(all_slots[:, :, None] == targets[None, None, :], axis=1).astype(jnp.bfloat16)

    def piece_gram(weights):
        picked = incoming * weights[:, None, None, None]
        left_side = lax.dynamic_slice_in_dim(picked, slab_pos * quarter_rows, quarter_rows, 3)
        gram_stiff = jnp.einsum(
            "smb,smc->bc", left_side[:, 0], incoming[:, 0], preferred_element_type=jnp.float32
        )
        gram_mass = jnp.einsum(
            "smb,smc->bc", left_side[:, 1], incoming[:, 1], preferred_element_type=jnp.float32
        )
        gram_mass = gram_mass - jnp.einsum(
            "smb,smc->bc", left_side[:, 2], incoming[:, 2], preferred_element_type=jnp.float32
        )
        return (gram_stiff, gram_mass)

    gram_k, gram_m = lax.map(piece_gram, select.T)
    return (interface_k + gram_k, interface_m + gram_m)


def body(subs, slabs, *arrays):
    adjacency = arrays[5]
    if adjacency.shape[1] == subs and subs % slabs == 0:
        return dense_body(subs, slabs, *arrays)
    return sparse_body(*arrays)


def solution(mesh):
    placed = (
        P("sub", "slab", None),
        P("sub", "slab", None),
        P("sub", "slab", None),
        P("sub", None, None),
        P("sub", None),
        P(),
        P(),
        P("sub", "slab", None),
        P("sub", "slab", None),
    )
    return jax.shard_map(
        functools.partial(body, mesh.shape["sub"], mesh.shape["slab"]),
        mesh=mesh,
        in_specs=placed,
        out_specs=(P("sub", "slab", None), P("sub", "slab", None)),
        check_vma=False,
    )
```

```python
import functools

import jax
import jax.numpy as jnp
from jax import lax
from jax.experimental import pallas as pl
from jax.experimental.pallas import tpu as pltpu
from jax.sharding import PartitionSpec as P

MESH = pl.DeviceIdType.MESH


def contract_rows(left, right):
    return lax.dot_general(
        left, right, (((0,), (0,)), ((), ())), preferred_element_type=jnp.float32
    )


def kernel(
    subs,
    slabs,
    adjacency_hbm,
    piece_slot_hbm,
    tile_range_hbm,
    eigenvalues_hbm,
    modes,
    coupling_k,
    coupling_m,
    gram,
    adjacency,
    piece_slot,
    tile_range,
    eigenvalues,
    my_modes,
    tile_k,
    tile_m,
    outgoing,
    columns,
    all_modes,
    blocks,
    arrived,
    small_sem,
    local_sem,
    modes_send,
    modes_recv,
    columns_send,
    columns_recv,
    blocks_send,
    blocks_recv,
):
    sub = lax.axis_index("sub")
    slab = lax.axis_index("slab")
    group = subs // slabs
    adj = adjacency.shape[1]
    _, owned, quarter, width = gram.shape
    rows = modes.shape[1]
    home = sub // group

    loads = [
        pltpu.make_async_copy(
            whole.at[0, :, a * width : (a + 1) * width], tile.at[a], local_sem.at[kind, a]
        )
        for a in range(adj)
        for kind, (whole, tile) in enumerate(((coupling_k, tile_k), (coupling_m, tile_m)))
    ]
    routing = [
        pltpu.make_async_copy(whole, held, small_sem.at[n])
        for n, (whole, held) in enumerate((
            (adjacency_hbm, adjacency), (piece_slot_hbm, piece_slot), (tile_range_hbm, tile_range)
        ))
    ]
    late = [
        pltpu.make_async_copy(whole, held, small_sem.at[3 + n])
        for n, (whole, held) in enumerate(((eigenvalues_hbm, eigenvalues),))
    ]
    late.append(pltpu.make_async_copy(modes.at[0], my_modes, small_sem.at[4]))
    for load in routing + late[1:] + loads:
        load.start()

    barrier = pltpu.get_barrier_semaphore()
    for turn in range(1, slabs):
        pl.semaphore_signal(
            barrier, inc=1, device_id=(sub, lax.rem(slab + turn, slabs)), device_id_type=MESH
        )
    for turn in range(1, subs):
        pl.semaphore_signal(
            barrier, inc=1, device_id=(lax.rem(sub + turn, subs), home), device_id_type=MESH
        )

    @pl.when(home != slab)
    def _():
        pl.semaphore_signal(barrier, inc=1, device_id=(sub, home), device_id_type=MESH)

    late[0].start()
    late[1].wait()
    half = rows // 2
    all_modes[slab] = jnp.concatenate([my_modes[:half], my_modes[half:]], axis=1)
    for load in routing:
        load.wait()
    slots = [piece_slot[adjacency[sub, a]] for a in range(adj)]

    def owner_of(part, step):
        return part * group + lax.rem(step + sub + 1, group)

    plan = []
    for step in range(group):
        for turn in list(range(1, slabs)) + [0]:
            owner = owner_of(lax.rem(slab + turn, slabs), step)
            place = jnp.int32(0)
            for a in range(adj):
                mine = (slots[a] >= owner * owned) & (slots[a] < (owner + 1) * owned)
                place = jnp.where(mine, jnp.int32(a), place)
            start = tile_range[0, 0, place] - slab * rows
            finish = tile_range[0, 1, place] - slab * rows
            plan.append((step, turn, place, start, finish))
    row_index = lax.broadcasted_iota(jnp.int32, (rows, width), 0)
    live = {}
    for step, turn, place, start, finish in plan:
        inside = (row_index >= start) & (row_index < finish)
        live[step, turn] = inside.astype(jnp.float32).astype(jnp.bfloat16)
    for load in loads:
        load.wait()

    def stage(wanted, kind):
        tile = (tile_k, tile_m)[kind]
        for step, turn, place, _, _ in plan:
            if step == wanted and turn > 0:
                outgoing[step, kind, turn - 1] = tile[place] * live[step, turn]

    sends = []

    def send_columns(step, kind):
        for turn in range(1, slabs):
            part = lax.rem(slab + turn, slabs)
            copy = pltpu.make_async_remote_copy(
                src_ref=outgoing.at[step, kind, turn - 1],
                dst_ref=columns.at[step, kind, slab],
                send_sem=columns_send.at[step, kind, turn - 1],
                recv_sem=columns_recv.at[step, kind, slab],
                device_id=(sub, part),
                device_id_type=MESH,
            )
            copy.start()
            sends.append(copy)

    stage(0, 0)

    @pl.when(home != slab)
    def _():
        pl.semaphore_wait(barrier, slabs - 1 + group * slabs)

    @pl.when(home == slab)
    def _():
        pl.semaphore_wait(barrier, slabs - 1 + group * slabs - 1)

    for turn in range(1, slabs):
        part = lax.rem(slab + turn, slabs)
        copy = pltpu.make_async_remote_copy(
            src_ref=all_modes.at[slab],
            dst_ref=all_modes.at[slab],
            send_sem=modes_send.at[turn - 1],
            recv_sem=modes_recv.at[slab],
            device_id=(sub, part),
            device_id_type=MESH,
        )
        copy.start()
        sends.append(copy)
    send_columns(0, 0)
    for step in range(group):
        for kind in range(2):
            if step + kind > 0:
                stage(step, kind)
                send_columns(step, kind)
    for step, turn, place, _, _ in plan:
        if turn == 0:
            columns[step, 0, slab] = tile_k[place] * live[step, 0]
            columns[step, 1, slab] = tile_m[place] * live[step, 0]

    takes = []
    for other in range(subs):
        theirs = [piece_slot[adjacency[other, a]] for a in range(adj)]
        takes.append([
            functools.reduce(
                lambda x, y: x | y,
                [(slot == sub * owned + q).astype(jnp.int32) for slot in theirs],
            )
            for q in range(owned)
        ])
    late[0].wait()
    eig = jnp.broadcast_to(eigenvalues[...], (width, modes.shape[2])).T
    root = lax.rsqrt(eig)

    for turn in range(1, slabs):
        part = lax.rem(slab + turn, slabs)
        pltpu.make_async_copy(all_modes.at[part], all_modes.at[part], modes_recv.at[part]).wait()
    mode_count = modes.shape[2]
    basis = jnp.concatenate([
        all_modes[part, :, side * mode_count : (side + 1) * mode_count]
        for part in range(slabs)
        for side in range(2)
    ]).T
    for step in range(group):
        owner = owner_of(slab, step)
        for kind in range(2):
            for turn in range(1, slabs):
                part = lax.rem(slab + turn, slabs)
                pltpu.make_async_copy(
                    columns.at[step, kind, part],
                    columns.at[step, kind, part],
                    columns_recv.at[step, kind, part],
                ).wait()
            proj = jnp.dot(
                basis,
                columns[step, kind].reshape(slabs * rows, width),
                preferred_element_type=jnp.float32,
            )
            if kind == 0:
                proj_s = proj
                first = (proj_s * root).astype(jnp.bfloat16)
                gram_part = contract_rows(first, first)
            else:
                second = (proj_s / eig - proj).astype(jnp.bfloat16)
                third = proj.astype(jnp.bfloat16)
                gram_part = contract_rows(
                    jnp.concatenate([second, third]), jnp.concatenate([second, -third])
                )
            blocks[step, kind] = gram_part.astype(jnp.bfloat16).reshape(slabs, quarter, width)
            for turn in range(1, slabs + 1):
                part = lax.rem(slab + turn, slabs)
                copy = pltpu.make_async_remote_copy(
                    src_ref=blocks.at[step, kind, part],
                    dst_ref=arrived.at[sub, kind],
                    send_sem=blocks_send.at[step, kind, turn - 1],
                    recv_sem=blocks_recv.at[sub, kind],
                    device_id=(owner, part),
                    device_id_type=MESH,
                )
                if turn < slabs:
                    copy.start()
                    sends.append(copy)
                else:
                    pl.when(owner != sub)(copy.start)

        @pl.when(owner == sub)
        def _():
            for kind in range(2):
                arrived[sub, kind] = blocks[step, kind, slab]

    for copy in sends:
        copy.wait_send()
    for step in range(group):

        @pl.when(owner_of(slab, step) != sub)
        def _():
            for kind in range(2):
                mine = blocks.at[step, kind, slab]
                pltpu.make_async_copy(mine, mine, blocks_send.at[step, kind, slabs - 1]).wait()

    total = [[jnp.zeros((quarter, width), jnp.float32)] * owned for _ in range(2)]
    for other in range(subs):

        @pl.when((other != sub) | (home != slab))
        def _():
            for kind in range(2):
                theirs = arrived.at[other, kind]
                pltpu.make_async_copy(theirs, theirs, blocks_recv.at[other, kind]).wait()

        for kind in range(2):
            term = arrived[other, kind].astype(jnp.float32)
            for q in range(owned):
                total[kind][q] = total[kind][q] + jnp.where(takes[other][q] > 0, term, 0.0)
    for q in range(owned):
        gram[0, q] = total[0][q]
        gram[1, q] = total[1][q]


def dense_body(
    subs,
    slabs,
    mode_shapes,
    coupling_k,
    coupling_m,
    tile_range,
    eigenvalues,
    adjacency,
    piece_slot,
    interface_k,
    interface_m,
):
    _, rows, mode_count = mode_shapes.shape
    adj = adjacency.shape[1]
    owned, quarter, width = interface_k.shape
    group = subs // slabs
    vmem = pl.BlockSpec(memory_space=pltpu.VMEM)
    hbm = pl.BlockSpec(memory_space=pltpu.HBM)
    gram = pl.pallas_call(
        functools.partial(kernel, subs, slabs),
        out_shape=jax.ShapeDtypeStruct((2,) + interface_k.shape, jnp.float32),
        in_specs=[hbm] * 7,
        out_specs=vmem,
        scratch_shapes=[
            pltpu.SMEM(adjacency.shape, adjacency.dtype),
            pltpu.SMEM(piece_slot.shape, piece_slot.dtype),
            pltpu.SMEM(tile_range.shape, tile_range.dtype),
            pltpu.VMEM(eigenvalues.shape, eigenvalues.dtype),
            pltpu.VMEM((rows, mode_count), jnp.bfloat16),
            pltpu.VMEM((adj, rows, width), jnp.bfloat16),
            pltpu.VMEM((adj, rows, width), jnp.bfloat16),
            pltpu.VMEM((group, 2, slabs - 1, rows, width), jnp.bfloat16),
            pltpu.VMEM((group, 2, slabs, rows, width), jnp.bfloat16),
            pltpu.VMEM((slabs, rows // 2, 2 * mode_count), jnp.bfloat16),
            pltpu.VMEM((group, 2, slabs, quarter, width), jnp.bfloat16),
            pltpu.VMEM((subs, 2, quarter, width), jnp.bfloat16),
            pltpu.SemaphoreType.DMA((5,)),
            pltpu.SemaphoreType.DMA((2, adj)),
            pltpu.SemaphoreType.DMA((slabs - 1,)),
            pltpu.SemaphoreType.DMA((slabs,)),
            pltpu.SemaphoreType.DMA((group, 2, slabs - 1)),
            pltpu.SemaphoreType.DMA((group, 2, slabs)),
            pltpu.SemaphoreType.DMA((group, 2, slabs)),
            pltpu.SemaphoreType.DMA((subs, 2)),
        ],
        compiler_params=pltpu.CompilerParams(
            collective_id=0, has_side_effects=True, vmem_limit_bytes=56 * 1024 * 1024
        ),
    )(
        adjacency,
        piece_slot,
        tile_range,
        eigenvalues,
        mode_shapes,
        coupling_k,
        coupling_m,
    )
    return (interface_k + gram[0], interface_m + gram[1])


def sparse_body(
    mode_shapes,
    coupling_k,
    coupling_m,
    tile_range,
    eigenvalues,
    adjacency,
    piece_slot,
    interface_k,
    interface_m,
):
    row_count = mode_shapes.shape[1]
    mode_count = mode_shapes.shape[2]
    adj_count = adjacency.shape[1]
    piece_width = interface_k.shape[2]
    owned_count = interface_k.shape[0]
    quarter_rows = interface_k.shape[1]
    sub_count = lax.axis_size("sub")
    slab_pos = lax.axis_index("slab")
    sub_pos = lax.axis_index("sub")
    row_index = slab_pos * row_count + lax.iota(jnp.int32, row_count)
    live = (
        (row_index[:, None] >= tile_range[0, 0][None, :])
        & (row_index[:, None] < tile_range[0, 1][None, :])
    ).astype(jnp.bfloat16)
    stiff_rows = (
        coupling_k[0].reshape(row_count, adj_count, piece_width) * live[:, :, None]
    ).reshape(row_count, adj_count * piece_width)
    mass_rows = (
        coupling_m[0].reshape(row_count, adj_count, piece_width) * live[:, :, None]
    ).reshape(row_count, adj_count * piece_width)
    part_s = jnp.einsum("rm,rc->mc", mode_shapes[0], stiff_rows, preferred_element_type=jnp.float32)
    part_v = jnp.einsum("rm,rc->mc", mode_shapes[0], mass_rows, preferred_element_type=jnp.float32)
    proj_s, proj_v = lax.psum((part_s, part_v), "slab")
    eig_held = eigenvalues[0]
    eig_col = eig_held[:, None]
    first = (proj_s * lax.rsqrt(eig_col)).astype(jnp.bfloat16)
    second = (proj_s / eig_col - proj_v).astype(jnp.bfloat16)
    third = proj_v.astype(jnp.bfloat16)
    stacked = jnp.stack([first, second, third]).reshape(3, mode_count, adj_count, piece_width)
    my_slots = piece_slot[adjacency[sub_pos]]
    owner_hot = (
        my_slots[None, :] // owned_count == lax.iota(jnp.int32, sub_count)[:, None]
    ).astype(jnp.bfloat16)
    outgoing = jnp.einsum(
        "oa,kmab->okmb", owner_hot, stacked, preferred_element_type=jnp.float32
    ).astype(jnp.bfloat16)
    incoming = lax.all_to_all(outgoing, "sub", split_axis=0, concat_axis=0, tiled=True)
    all_slots = piece_slot[adjacency]
    targets = sub_pos * owned_count + lax.iota(jnp.int32, owned_count)
    select = jnp.any(all_slots[:, :, None] == targets[None, None, :], axis=1).astype(jnp.bfloat16)

    def piece_gram(weights):
        picked = incoming * weights[:, None, None, None]
        left_side = lax.dynamic_slice_in_dim(picked, slab_pos * quarter_rows, quarter_rows, 3)
        gram_stiff = jnp.einsum(
            "smb,smc->bc", left_side[:, 0], incoming[:, 0], preferred_element_type=jnp.float32
        )
        gram_mass = jnp.einsum(
            "smb,smc->bc", left_side[:, 1], incoming[:, 1], preferred_element_type=jnp.float32
        )
        gram_mass = gram_mass - jnp.einsum(
            "smb,smc->bc", left_side[:, 2], incoming[:, 2], preferred_element_type=jnp.float32
        )
        return (gram_stiff, gram_mass)

    gram_k, gram_m = lax.map(piece_gram, select.T)
    return (interface_k + gram_k, interface_m + gram_m)


def body(subs, slabs, *arrays):
    adjacency = arrays[5]
    if adjacency.shape[1] == subs and subs % slabs == 0:
        return dense_body(subs, slabs, *arrays)
    return sparse_body(*arrays)


def solution(mesh):
    placed = (
        P("sub", "slab", None),
        P("sub", "slab", None),
        P("sub", "slab", None),
        P("sub", None, None),
        P("sub", None),
        P(),
        P(),
        P("sub", "slab", None),
        P("sub", "slab", None),
    )
    return jax.shard_map(
        functools.partial(body, mesh.shape["sub"], mesh.shape["slab"]),
        mesh=mesh,
        in_specs=placed,
        out_specs=(P("sub", "slab", None), P("sub", "slab", None)),
        check_vma=False,
    )
```

```python
import functools

import jax
import jax.numpy as jnp
from jax import lax
from jax.experimental import pallas as pl
from jax.experimental.pallas import tpu as pltpu
from jax.sharding import PartitionSpec as P

MESH = pl.DeviceIdType.MESH


def contract_rows(left, right):
    return lax.dot_general(
        left, right, (((0,), (0,)), ((), ())), preferred_element_type=jnp.float32
    )


def kernel(
    subs,
    slabs,
    adjacency_hbm,
    piece_slot_hbm,
    tile_range_hbm,
    eigenvalues_hbm,
    modes,
    coupling_k,
    coupling_m,
    gram,
    adjacency,
    piece_slot,
    tile_range,
    eigenvalues,
    my_modes,
    tile_k,
    tile_m,
    outgoing,
    columns,
    all_modes,
    blocks,
    arrived,
    small_sem,
    local_sem,
    modes_send,
    modes_recv,
    columns_send,
    columns_recv,
    blocks_send,
    blocks_recv,
):
    sub = lax.axis_index("sub")
    slab = lax.axis_index("slab")
    group = subs // slabs
    adj = adjacency.shape[1]
    _, owned, quarter, width = gram.shape
    rows = modes.shape[1]
    home = sub // group

    loads = [
        pltpu.make_async_copy(
            whole.at[0, :, a * width : (a + 1) * width], tile.at[a], local_sem.at[kind, a]
        )
        for a in range(adj)
        for kind, (whole, tile) in enumerate(((coupling_k, tile_k), (coupling_m, tile_m)))
    ]
    routing = [
        pltpu.make_async_copy(whole, held, small_sem.at[n])
        for n, (whole, held) in enumerate((
            (adjacency_hbm, adjacency), (piece_slot_hbm, piece_slot), (tile_range_hbm, tile_range)
        ))
    ]
    late = [
        pltpu.make_async_copy(whole, held, small_sem.at[3 + n])
        for n, (whole, held) in enumerate(((eigenvalues_hbm, eigenvalues),))
    ]
    late.append(pltpu.make_async_copy(modes.at[0], my_modes, small_sem.at[4]))
    for load in routing + late[1:] + loads:
        load.start()

    barrier = pltpu.get_barrier_semaphore()
    for turn in range(1, slabs):
        pl.semaphore_signal(
            barrier, inc=1, device_id=(sub, lax.rem(slab + turn, slabs)), device_id_type=MESH
        )
    for turn in range(1, subs):
        pl.semaphore_signal(
            barrier, inc=1, device_id=(lax.rem(sub + turn, subs), home), device_id_type=MESH
        )

    @pl.when(home != slab)
    def _():
        pl.semaphore_signal(barrier, inc=1, device_id=(sub, home), device_id_type=MESH)

    late[0].start()
    late[1].wait()
    half = rows // 2
    all_modes[slab] = jnp.concatenate([my_modes[:half], my_modes[half:]], axis=1)
    for load in routing:
        load.wait()
    slots = [piece_slot[adjacency[sub, a]] for a in range(adj)]

    def owner_of(part, step):
        return part * group + lax.rem(step + sub + 1, group)

    plan = []
    for step in range(group):
        for turn in list(range(1, slabs)) + [0]:
            owner = owner_of(lax.rem(slab + turn, slabs), step)
            place = jnp.int32(0)
            for a in range(adj):
                mine = (slots[a] >= owner * owned) & (slots[a] < (owner + 1) * owned)
                place = jnp.where(mine, jnp.int32(a), place)
            start = tile_range[0, 0, place] - slab * rows
            finish = tile_range[0, 1, place] - slab * rows
            plan.append((step, turn, place, start, finish))
    row_index = lax.broadcasted_iota(jnp.int32, (rows, width), 0)
    live = {}
    for step, turn, place, start, finish in plan:
        inside = (row_index >= start) & (row_index < finish)
        live[step, turn] = inside.astype(jnp.float32).astype(jnp.bfloat16)
    for load in loads:
        load.wait()

    def stage(wanted, kind):
        tile = (tile_k, tile_m)[kind]
        for step, turn, place, _, _ in plan:
            if step == wanted and turn > 0:
                outgoing[step, kind, turn - 1] = tile[place] * live[step, turn]

    sends = []

    def send_columns(step, kind):
        for turn in range(1, slabs):
            part = lax.rem(slab + turn, slabs)
            copy = pltpu.make_async_remote_copy(
                src_ref=outgoing.at[step, kind, turn - 1],
                dst_ref=columns.at[step, kind, slab],
                send_sem=columns_send.at[step, kind, turn - 1],
                recv_sem=columns_recv.at[step, kind, slab],
                device_id=(sub, part),
                device_id_type=MESH,
            )
            copy.start()
            sends.append(copy)

    stage(0, 0)

    @pl.when(home != slab)
    def _():
        pl.semaphore_wait(barrier, slabs - 1 + group * slabs)

    @pl.when(home == slab)
    def _():
        pl.semaphore_wait(barrier, slabs - 1 + group * slabs - 1)

    for turn in range(1, slabs):
        part = lax.rem(slab + turn, slabs)
        copy = pltpu.make_async_remote_copy(
            src_ref=all_modes.at[slab],
            dst_ref=all_modes.at[slab],
            send_sem=modes_send.at[turn - 1],
            recv_sem=modes_recv.at[slab],
            device_id=(sub, part),
            device_id_type=MESH,
        )
        copy.start()
        sends.append(copy)
    send_columns(0, 0)
    for step in range(group):
        for kind in range(2):
            if step + kind > 0:
                stage(step, kind)
                send_columns(step, kind)
    for step, turn, place, _, _ in plan:
        if turn == 0:
            columns[step, 0, slab] = tile_k[place] * live[step, 0]
            columns[step, 1, slab] = tile_m[place] * live[step, 0]

    takes = []
    for other in range(subs):
        theirs = [piece_slot[adjacency[other, a]] for a in range(adj)]
        takes.append([
            functools.reduce(
                lambda x, y: x | y,
                [(slot == sub * owned + q).astype(jnp.int32) for slot in theirs],
            )
            for q in range(owned)
        ])
    late[0].wait()
    eig = jnp.broadcast_to(eigenvalues[...], (width, modes.shape[2])).T
    root = lax.rsqrt(eig)

    for turn in range(1, slabs):
        part = lax.rem(slab + turn, slabs)
        pltpu.make_async_copy(all_modes.at[part], all_modes.at[part], modes_recv.at[part]).wait()
    mode_count = modes.shape[2]
    basis = jnp.concatenate([
        all_modes[part, :, side * mode_count : (side + 1) * mode_count]
        for part in range(slabs)
        for side in range(2)
    ]).T
    for step in range(group):
        owner = owner_of(slab, step)
        for kind in range(2):
            for turn in range(1, slabs):
                part = lax.rem(slab + turn, slabs)
                pltpu.make_async_copy(
                    columns.at[step, kind, part],
                    columns.at[step, kind, part],
                    columns_recv.at[step, kind, part],
                ).wait()
            proj = jnp.dot(
                basis,
                columns[step, kind].reshape(slabs * rows, width),
                preferred_element_type=jnp.float32,
            )
            if kind == 0:
                proj_s = proj
                first = (proj_s * root).astype(jnp.bfloat16)
                gram_part = contract_rows(first, first)
            else:
                second = (proj_s / eig - proj).astype(jnp.bfloat16)
                third = proj.astype(jnp.bfloat16)
                gram_part = contract_rows(
                    jnp.concatenate([second, third]), jnp.concatenate([second, -third])
                )
            blocks[step, kind] = gram_part.astype(jnp.bfloat16).reshape(slabs, quarter, width)
            for turn in range(1, slabs + 1):
                part = lax.rem(slab + turn, slabs)
                copy = pltpu.make_async_remote_copy(
                    src_ref=blocks.at[step, kind, part],
                    dst_ref=arrived.at[sub, kind],
                    send_sem=blocks_send.at[step, kind, turn - 1],
                    recv_sem=blocks_recv.at[sub, kind],
                    device_id=(owner, part),
                    device_id_type=MESH,
                )
                if turn < slabs:
                    copy.start()
                    sends.append(copy)
                else:
                    pl.when(owner != sub)(copy.start)

        @pl.when(owner == sub)
        def _():
            for kind in range(2):
                arrived[sub, kind] = blocks[step, kind, slab]

    for copy in sends:
        copy.wait_send()
    for step in range(group):

        @pl.when(owner_of(slab, step) != sub)
        def _():
            for kind in range(2):
                mine = blocks.at[step, kind, slab]
                pltpu.make_async_copy(mine, mine, blocks_send.at[step, kind, slabs - 1]).wait()

    total = [[jnp.zeros((quarter, width), jnp.float32)] * owned for _ in range(2)]
    for other in range(subs):

        @pl.when((other != sub) | (home != slab))
        def _():
            for kind in range(2):
                theirs = arrived.at[other, kind]
                pltpu.make_async_copy(theirs, theirs, blocks_recv.at[other, kind]).wait()

        for kind in range(2):
            term = arrived[other, kind].astype(jnp.float32)
            for q in range(owned):
                total[kind][q] = total[kind][q] + jnp.where(takes[other][q] > 0, term, 0.0)
    for q in range(owned):
        gram[0, q] = total[0][q]
        gram[1, q] = total[1][q]


def dense_body(
    subs,
    slabs,
    mode_shapes,
    coupling_k,
    coupling_m,
    tile_range,
    eigenvalues,
    adjacency,
    piece_slot,
    interface_k,
    interface_m,
):
    _, rows, mode_count = mode_shapes.shape
    adj = adjacency.shape[1]
    owned, quarter, width = interface_k.shape
    group = subs // slabs
    vmem = pl.BlockSpec(memory_space=pltpu.VMEM)
    hbm = pl.BlockSpec(memory_space=pltpu.HBM)
    gram = pl.pallas_call(
        functools.partial(kernel, subs, slabs),
        out_shape=pltpu.VMEM((2,) + interface_k.shape, jnp.float32),
        in_specs=[hbm] * 7,
        out_specs=vmem,
        scratch_shapes=[
            pltpu.SMEM(adjacency.shape, adjacency.dtype),
            pltpu.SMEM(piece_slot.shape, piece_slot.dtype),
            pltpu.SMEM(tile_range.shape, tile_range.dtype),
            pltpu.VMEM(eigenvalues.shape, eigenvalues.dtype),
            pltpu.VMEM((rows, mode_count), jnp.bfloat16),
            pltpu.VMEM((adj, rows, width), jnp.bfloat16),
            pltpu.VMEM((adj, rows, width), jnp.bfloat16),
            pltpu.VMEM((group, 2, slabs - 1, rows, width), jnp.bfloat16),
            pltpu.VMEM((group, 2, slabs, rows, width), jnp.bfloat16),
            pltpu.VMEM((slabs, rows // 2, 2 * mode_count), jnp.bfloat16),
            pltpu.VMEM((group, 2, slabs, quarter, width), jnp.bfloat16),
            pltpu.VMEM((subs, 2, quarter, width), jnp.bfloat16),
            pltpu.SemaphoreType.DMA((5,)),
            pltpu.SemaphoreType.DMA((2, adj)),
            pltpu.SemaphoreType.DMA((slabs - 1,)),
            pltpu.SemaphoreType.DMA((slabs,)),
            pltpu.SemaphoreType.DMA((group, 2, slabs - 1)),
            pltpu.SemaphoreType.DMA((group, 2, slabs)),
            pltpu.SemaphoreType.DMA((group, 2, slabs)),
            pltpu.SemaphoreType.DMA((subs, 2)),
        ],
        compiler_params=pltpu.CompilerParams(
            collective_id=0, has_side_effects=True, vmem_limit_bytes=56 * 1024 * 1024
        ),
    )(
        adjacency,
        piece_slot,
        tile_range,
        eigenvalues,
        mode_shapes,
        coupling_k,
        coupling_m,
    )
    return (interface_k + gram[0], interface_m + gram[1])


def sparse_body(
    mode_shapes,
    coupling_k,
    coupling_m,
    tile_range,
    eigenvalues,
    adjacency,
    piece_slot,
    interface_k,
    interface_m,
):
    row_count = mode_shapes.shape[1]
    mode_count = mode_shapes.shape[2]
    adj_count = adjacency.shape[1]
    piece_width = interface_k.shape[2]
    owned_count = interface_k.shape[0]
    quarter_rows = interface_k.shape[1]
    sub_count = lax.axis_size("sub")
    slab_pos = lax.axis_index("slab")
    sub_pos = lax.axis_index("sub")
    row_index = slab_pos * row_count + lax.iota(jnp.int32, row_count)
    live = (
        (row_index[:, None] >= tile_range[0, 0][None, :])
        & (row_index[:, None] < tile_range[0, 1][None, :])
    ).astype(jnp.bfloat16)
    stiff_rows = (
        coupling_k[0].reshape(row_count, adj_count, piece_width) * live[:, :, None]
    ).reshape(row_count, adj_count * piece_width)
    mass_rows = (
        coupling_m[0].reshape(row_count, adj_count, piece_width) * live[:, :, None]
    ).reshape(row_count, adj_count * piece_width)
    part_s = jnp.einsum("rm,rc->mc", mode_shapes[0], stiff_rows, preferred_element_type=jnp.float32)
    part_v = jnp.einsum("rm,rc->mc", mode_shapes[0], mass_rows, preferred_element_type=jnp.float32)
    proj_s, proj_v = lax.psum((part_s, part_v), "slab")
    eig_held = eigenvalues[0]
    eig_col = eig_held[:, None]
    first = (proj_s * lax.rsqrt(eig_col)).astype(jnp.bfloat16)
    second = (proj_s / eig_col - proj_v).astype(jnp.bfloat16)
    third = proj_v.astype(jnp.bfloat16)
    stacked = jnp.stack([first, second, third]).reshape(3, mode_count, adj_count, piece_width)
    my_slots = piece_slot[adjacency[sub_pos]]
    owner_hot = (
        my_slots[None, :] // owned_count == lax.iota(jnp.int32, sub_count)[:, None]
    ).astype(jnp.bfloat16)
    outgoing = jnp.einsum(
        "oa,kmab->okmb", owner_hot, stacked, preferred_element_type=jnp.float32
    ).astype(jnp.bfloat16)
    incoming = lax.all_to_all(outgoing, "sub", split_axis=0, concat_axis=0, tiled=True)
    all_slots = piece_slot[adjacency]
    targets = sub_pos * owned_count + lax.iota(jnp.int32, owned_count)
    select = jnp.any(all_slots[:, :, None] == targets[None, None, :], axis=1).astype(jnp.bfloat16)

    def piece_gram(weights):
        picked = incoming * weights[:, None, None, None]
        left_side = lax.dynamic_slice_in_dim(picked, slab_pos * quarter_rows, quarter_rows, 3)
        gram_stiff = jnp.einsum(
            "smb,smc->bc", left_side[:, 0], incoming[:, 0], preferred_element_type=jnp.float32
        )
        gram_mass = jnp.einsum(
            "smb,smc->bc", left_side[:, 1], incoming[:, 1], preferred_element_type=jnp.float32
        )
        gram_mass = gram_mass - jnp.einsum(
            "smb,smc->bc", left_side[:, 2], incoming[:, 2], preferred_element_type=jnp.float32
        )
        return (gram_stiff, gram_mass)

    gram_k, gram_m = lax.map(piece_gram, select.T)
    return (interface_k + gram_k, interface_m + gram_m)


def body(subs, slabs, *arrays):
    adjacency = arrays[5]
    if adjacency.shape[1] == subs and subs % slabs == 0:
        return dense_body(subs, slabs, *arrays)
    return sparse_body(*arrays)


def solution(mesh):
    placed = (
        P("sub", "slab", None),
        P("sub", "slab", None),
        P("sub", "slab", None),
        P("sub", None, None),
        P("sub", None),
        P(),
        P(),
        P("sub", "slab", None),
        P("sub", "slab", None),
    )
    return jax.shard_map(
        functools.partial(body, mesh.shape["sub"], mesh.shape["slab"]),
        mesh=mesh,
        in_specs=placed,
        out_specs=(P("sub", "slab", None), P("sub", "slab", None)),
        check_vma=False,
    )
```

```python
import functools

import jax
import jax.numpy as jnp
from jax import lax
from jax.experimental import pallas as pl
from jax.experimental.pallas import tpu as pltpu
from jax.sharding import PartitionSpec as P

MESH = pl.DeviceIdType.MESH


def contract_rows(left, right):
    return lax.dot_general(
        left, right, (((0,), (0,)), ((), ())), preferred_element_type=jnp.float32
    )


def kernel(
    subs,
    slabs,
    adjacency_hbm,
    piece_slot_hbm,
    tile_range_hbm,
    eigenvalues_hbm,
    modes,
    coupling_k,
    coupling_m,
    gram,
    adjacency,
    piece_slot,
    tile_range,
    eigenvalues,
    my_modes,
    tile_k,
    tile_m,
    outgoing,
    columns,
    all_modes,
    blocks,
    arrived,
    small_sem,
    local_sem,
    modes_send,
    modes_recv,
    columns_send,
    columns_recv,
    blocks_send,
    blocks_recv,
):
    sub = lax.axis_index("sub")
    slab = lax.axis_index("slab")
    group = subs // slabs
    adj = adjacency.shape[1]
    _, owned, quarter, width = gram.shape
    rows = modes.shape[1]
    home = sub // group

    loads_k, loads_m = [
        [
            pltpu.make_async_copy(
                whole.at[0, :, a * width : (a + 1) * width], tile.at[a], local_sem.at[kind, a]
            )
            for a in range(adj)
        ]
        for kind, (whole, tile) in enumerate(((coupling_k, tile_k), (coupling_m, tile_m)))
    ]
    routing = [
        pltpu.make_async_copy(whole, held, small_sem.at[n])
        for n, (whole, held) in enumerate((
            (adjacency_hbm, adjacency), (piece_slot_hbm, piece_slot), (tile_range_hbm, tile_range)
        ))
    ]
    late = [
        pltpu.make_async_copy(whole, held, small_sem.at[3 + n])
        for n, (whole, held) in enumerate(((eigenvalues_hbm, eigenvalues),))
    ]
    late.append(pltpu.make_async_copy(modes.at[0], my_modes, small_sem.at[4]))
    for load in routing + loads_k + late[1:]:
        load.start()

    barrier = pltpu.get_barrier_semaphore()
    for turn in range(1, slabs):
        pl.semaphore_signal(
            barrier, inc=1, device_id=(sub, lax.rem(slab + turn, slabs)), device_id_type=MESH
        )
    for turn in range(1, subs):
        pl.semaphore_signal(
            barrier, inc=1, device_id=(lax.rem(sub + turn, subs), home), device_id_type=MESH
        )

    @pl.when(home != slab)
    def _():
        pl.semaphore_signal(barrier, inc=1, device_id=(sub, home), device_id_type=MESH)

    for load in loads_m + late[:1]:
        load.start()
    for load in routing:
        load.wait()
    slots = [piece_slot[adjacency[sub, a]] for a in range(adj)]

    def owner_of(part, step):
        return part * group + lax.rem(step + sub + 1, group)

    plan = []
    for step in range(group):
        for turn in list(range(1, slabs)) + [0]:
            owner = owner_of(lax.rem(slab + turn, slabs), step)
            place = jnp.int32(0)
            for a in range(adj):
                mine = (slots[a] >= owner * owned) & (slots[a] < (owner + 1) * owned)
                place = jnp.where(mine, jnp.int32(a), place)
            start = tile_range[0, 0, place] - slab * rows
            finish = tile_range[0, 1, place] - slab * rows
            plan.append((step, turn, place, start, finish))
    row_index = lax.broadcasted_iota(jnp.int32, (rows, width), 0)
    live = {}
    for step, turn, place, start, finish in plan:
        inside = (row_index >= start) & (row_index < finish)
        live[step, turn] = inside.astype(jnp.float32).astype(jnp.bfloat16)
    for load in loads_k:
        load.wait()

    def stage(wanted, kind):
        tile = (tile_k, tile_m)[kind]
        for step, turn, place, _, _ in plan:
            if step == wanted and turn > 0:
                outgoing[step, kind, turn - 1] = tile[place] * live[step, turn]

    sends = []

    def send_columns(step, kind):
        for turn in range(1, slabs):
            part = lax.rem(slab + turn, slabs)
            copy = pltpu.make_async_remote_copy(
                src_ref=outgoing.at[step, kind, turn - 1],
                dst_ref=columns.at[step, kind, slab],
                send_sem=columns_send.at[step, kind, turn - 1],
                recv_sem=columns_recv.at[step, kind, slab],
                device_id=(sub, part),
                device_id_type=MESH,
            )
            copy.start()
            sends.append(copy)

    stage(0, 0)
    late[1].wait()
    half = rows // 2
    all_modes[slab] = jnp.concatenate([my_modes[:half], my_modes[half:]], axis=1)

    @pl.when(home != slab)
    def _():
        pl.semaphore_wait(barrier, slabs - 1 + group * slabs)

    @pl.when(home == slab)
    def _():
        pl.semaphore_wait(barrier, slabs - 1 + group * slabs - 1)

    for turn in range(1, slabs):
        part = lax.rem(slab + turn, slabs)
        copy = pltpu.make_async_remote_copy(
            src_ref=all_modes.at[slab],
            dst_ref=all_modes.at[slab],
            send_sem=modes_send.at[turn - 1],
            recv_sem=modes_recv.at[slab],
            device_id=(sub, part),
            device_id_type=MESH,
        )
        copy.start()
        sends.append(copy)
    send_columns(0, 0)
    for load in loads_m:
        load.wait()
    for step in range(group):
        for kind in range(2):
            if step + kind > 0:
                stage(step, kind)
                send_columns(step, kind)
    for step, turn, place, _, _ in plan:
        if turn == 0:
            columns[step, 0, slab] = tile_k[place] * live[step, 0]
            columns[step, 1, slab] = tile_m[place] * live[step, 0]

    takes = []
    for other in range(subs):
        theirs = [piece_slot[adjacency[other, a]] for a in range(adj)]
        takes.append([
            functools.reduce(
                lambda x, y: x | y,
                [(slot == sub * owned + q).astype(jnp.int32) for slot in theirs],
            )
            for q in range(owned)
        ])
    late[0].wait()
    eig = jnp.broadcast_to(eigenvalues[...], (width, modes.shape[2])).T
    root = lax.rsqrt(eig)

    for turn in range(1, slabs):
        part = lax.rem(slab + turn, slabs)
        pltpu.make_async_copy(all_modes.at[part], all_modes.at[part], modes_recv.at[part]).wait()
    mode_count = modes.shape[2]
    basis = jnp.concatenate([
        all_modes[part, :, side * mode_count : (side + 1) * mode_count]
        for part in range(slabs)
        for side in range(2)
    ]).T
    for step in range(group):
        owner = owner_of(slab, step)
        for kind in range(2):
            for turn in range(1, slabs):
                part = lax.rem(slab + turn, slabs)
                pltpu.make_async_copy(
                    columns.at[step, kind, part],
                    columns.at[step, kind, part],
                    columns_recv.at[step, kind, part],
                ).wait()
            proj = jnp.dot(
                basis,
                columns[step, kind].reshape(slabs * rows, width),
                preferred_element_type=jnp.float32,
            )
            if kind == 0:
                ratio = proj / eig
                first = (proj * root).astype(jnp.bfloat16)
                gram_part = contract_rows(first, first)
            else:
                second = (ratio - proj).astype(jnp.bfloat16)
                third = proj.astype(jnp.bfloat16)
                gram_part = contract_rows(
                    jnp.concatenate([second, third]), jnp.concatenate([second, -third])
                )
            blocks[step, kind] = gram_part.astype(jnp.bfloat16).reshape(slabs, quarter, width)
            for turn in range(1, slabs + 1):
                part = lax.rem(slab + turn, slabs)
                copy = pltpu.make_async_remote_copy(
                    src_ref=blocks.at[step, kind, part],
                    dst_ref=arrived.at[sub, kind],
                    send_sem=blocks_send.at[step, kind, turn - 1],
                    recv_sem=blocks_recv.at[sub, kind],
                    device_id=(owner, part),
                    device_id_type=MESH,
                )
                if turn < slabs:
                    copy.start()
                    sends.append(copy)
                else:
                    pl.when(owner != sub)(copy.start)

        @pl.when(owner == sub)
        def _():
            for kind in range(2):
                arrived[sub, kind] = blocks[step, kind, slab]

    for copy in sends:
        copy.wait_send()
    for step in range(group):

        @pl.when(owner_of(slab, step) != sub)
        def _():
            for kind in range(2):
                mine = blocks.at[step, kind, slab]
                pltpu.make_async_copy(mine, mine, blocks_send.at[step, kind, slabs - 1]).wait()

    total = [[jnp.zeros((quarter, width), jnp.float32)] * owned for _ in range(2)]
    for other in range(subs):

        @pl.when((other != sub) | (home != slab))
        def _():
            for kind in range(2):
                theirs = arrived.at[other, kind]
                pltpu.make_async_copy(theirs, theirs, blocks_recv.at[other, kind]).wait()

        for kind in range(2):
            term = arrived[other, kind].astype(jnp.float32)
            for q in range(owned):
                total[kind][q] = total[kind][q] + jnp.where(takes[other][q] > 0, term, 0.0)
    for q in range(owned):
        gram[0, q] = total[0][q]
        gram[1, q] = total[1][q]


def dense_body(
    subs,
    slabs,
    mode_shapes,
    coupling_k,
    coupling_m,
    tile_range,
    eigenvalues,
    adjacency,
    piece_slot,
    interface_k,
    interface_m,
):
    _, rows, mode_count = mode_shapes.shape
    adj = adjacency.shape[1]
    owned, quarter, width = interface_k.shape
    group = subs // slabs
    vmem = pl.BlockSpec(memory_space=pltpu.VMEM)
    hbm = pl.BlockSpec(memory_space=pltpu.HBM)
    gram = pl.pallas_call(
        functools.partial(kernel, subs, slabs),
        out_shape=pltpu.VMEM((2,) + interface_k.shape, jnp.float32),
        in_specs=[hbm] * 7,
        out_specs=vmem,
        scratch_shapes=[
            pltpu.SMEM(adjacency.shape, adjacency.dtype),
            pltpu.SMEM(piece_slot.shape, piece_slot.dtype),
            pltpu.SMEM(tile_range.shape, tile_range.dtype),
            pltpu.VMEM(eigenvalues.shape, eigenvalues.dtype),
            pltpu.VMEM((rows, mode_count), jnp.bfloat16),
            pltpu.VMEM((adj, rows, width), jnp.bfloat16),
            pltpu.VMEM((adj, rows, width), jnp.bfloat16),
            pltpu.VMEM((group, 2, slabs - 1, rows, width), jnp.bfloat16),
            pltpu.VMEM((group, 2, slabs, rows, width), jnp.bfloat16),
            pltpu.VMEM((slabs, rows // 2, 2 * mode_count), jnp.bfloat16),
            pltpu.VMEM((group, 2, slabs, quarter, width), jnp.bfloat16),
            pltpu.VMEM((subs, 2, quarter, width), jnp.bfloat16),
            pltpu.SemaphoreType.DMA((5,)),
            pltpu.SemaphoreType.DMA((2, adj)),
            pltpu.SemaphoreType.DMA((slabs - 1,)),
            pltpu.SemaphoreType.DMA((slabs,)),
            pltpu.SemaphoreType.DMA((group, 2, slabs - 1)),
            pltpu.SemaphoreType.DMA((group, 2, slabs)),
            pltpu.SemaphoreType.DMA((group, 2, slabs)),
            pltpu.SemaphoreType.DMA((subs, 2)),
        ],
        compiler_params=pltpu.CompilerParams(
            collective_id=0, has_side_effects=True, vmem_limit_bytes=56 * 1024 * 1024
        ),
    )(
        adjacency,
        piece_slot,
        tile_range,
        eigenvalues,
        mode_shapes,
        coupling_k,
        coupling_m,
    )
    return (interface_k + gram[0], interface_m + gram[1])


def sparse_body(
    mode_shapes,
    coupling_k,
    coupling_m,
    tile_range,
    eigenvalues,
    adjacency,
    piece_slot,
    interface_k,
    interface_m,
):
    row_count = mode_shapes.shape[1]
    mode_count = mode_shapes.shape[2]
    adj_count = adjacency.shape[1]
    piece_width = interface_k.shape[2]
    owned_count = interface_k.shape[0]
    quarter_rows = interface_k.shape[1]
    sub_count = lax.axis_size("sub")
    slab_pos = lax.axis_index("slab")
    sub_pos = lax.axis_index("sub")
    row_index = slab_pos * row_count + lax.iota(jnp.int32, row_count)
    live = (
        (row_index[:, None] >= tile_range[0, 0][None, :])
        & (row_index[:, None] < tile_range[0, 1][None, :])
    ).astype(jnp.bfloat16)
    stiff_rows = (
        coupling_k[0].reshape(row_count, adj_count, piece_width) * live[:, :, None]
    ).reshape(row_count, adj_count * piece_width)
    mass_rows = (
        coupling_m[0].reshape(row_count, adj_count, piece_width) * live[:, :, None]
    ).reshape(row_count, adj_count * piece_width)
    part_s = jnp.einsum("rm,rc->mc", mode_shapes[0], stiff_rows, preferred_element_type=jnp.float32)
    part_v = jnp.einsum("rm,rc->mc", mode_shapes[0], mass_rows, preferred_element_type=jnp.float32)
    proj_s, proj_v = lax.psum((part_s, part_v), "slab")
    eig_held = eigenvalues[0]
    eig_col = eig_held[:, None]
    first = (proj_s * lax.rsqrt(eig_col)).astype(jnp.bfloat16)
    second = (proj_s / eig_col - proj_v).astype(jnp.bfloat16)
    third = proj_v.astype(jnp.bfloat16)
    stacked = jnp.stack([first, second, third]).reshape(3, mode_count, adj_count, piece_width)
    my_slots = piece_slot[adjacency[sub_pos]]
    owner_hot = (
        my_slots[None, :] // owned_count == lax.iota(jnp.int32, sub_count)[:, None]
    ).astype(jnp.bfloat16)
    outgoing = jnp.einsum(
        "oa,kmab->okmb", owner_hot, stacked, preferred_element_type=jnp.float32
    ).astype(jnp.bfloat16)
    incoming = lax.all_to_all(outgoing, "sub", split_axis=0, concat_axis=0, tiled=True)
    all_slots = piece_slot[adjacency]
    targets = sub_pos * owned_count + lax.iota(jnp.int32, owned_count)
    select = jnp.any(all_slots[:, :, None] == targets[None, None, :], axis=1).astype(jnp.bfloat16)

    def piece_gram(weights):
        picked = incoming * weights[:, None, None, None]
        left_side = lax.dynamic_slice_in_dim(picked, slab_pos * quarter_rows, quarter_rows, 3)
        gram_stiff = jnp.einsum(
            "smb,smc->bc", left_side[:, 0], incoming[:, 0], preferred_element_type=jnp.float32
        )
        gram_mass = jnp.einsum(
            "smb,smc->bc", left_side[:, 1], incoming[:, 1], preferred_element_type=jnp.float32
        )
        gram_mass = gram_mass - jnp.einsum(
            "smb,smc->bc", left_side[:, 2], incoming[:, 2], preferred_element_type=jnp.float32
        )
        return (gram_stiff, gram_mass)

    gram_k, gram_m = lax.map(piece_gram, select.T)
    return (interface_k + gram_k, interface_m + gram_m)


def body(subs, slabs, *arrays):
    adjacency = arrays[5]
    if adjacency.shape[1] == subs and subs % slabs == 0:
        return dense_body(subs, slabs, *arrays)
    return sparse_body(*arrays)


def solution(mesh):
    placed = (
        P("sub", "slab", None),
        P("sub", "slab", None),
        P("sub", "slab", None),
        P("sub", None, None),
        P("sub", None),
        P(),
        P(),
        P("sub", "slab", None),
        P("sub", "slab", None),
    )
    return jax.shard_map(
        functools.partial(body, mesh.shape["sub"], mesh.shape["slab"]),
        mesh=mesh,
        in_specs=placed,
        out_specs=(P("sub", "slab", None), P("sub", "slab", None)),
        check_vma=False,
    )
```

```python
import functools

import jax
import jax.numpy as jnp
from jax import lax
from jax.experimental import pallas as pl
from jax.experimental.pallas import tpu as pltpu
from jax.sharding import PartitionSpec as P

MESH = pl.DeviceIdType.MESH


def contract_rows(left, right):
    return lax.dot_general(
        left, right, (((0,), (0,)), ((), ())), preferred_element_type=jnp.float32
    )


def kernel(
    subs,
    slabs,
    adjacency_hbm,
    piece_slot_hbm,
    tile_range_hbm,
    eigenvalues_hbm,
    modes,
    coupling_k,
    coupling_m,
    gram,
    adjacency,
    piece_slot,
    tile_range,
    eigenvalues,
    my_modes,
    tile_k,
    tile_m,
    outgoing,
    columns,
    all_modes,
    blocks,
    arrived,
    small_sem,
    local_sem,
    modes_send,
    modes_recv,
    columns_send,
    columns_recv,
    blocks_send,
    blocks_recv,
):
    sub = lax.axis_index("sub")
    slab = lax.axis_index("slab")
    group = subs // slabs
    adj = adjacency.shape[1]
    _, owned, quarter, width = gram.shape
    rows = modes.shape[1]
    home = sub // group

    loads_k, loads_m = [
        [
            pltpu.make_async_copy(
                whole.at[0, :, a * width : (a + 1) * width], tile.at[a], local_sem.at[kind, a]
            )
            for a in range(adj)
        ]
        for kind, (whole, tile) in enumerate(((coupling_k, tile_k), (coupling_m, tile_m)))
    ]
    routing = [
        pltpu.make_async_copy(whole, held, small_sem.at[n])
        for n, (whole, held) in enumerate((
            (adjacency_hbm, adjacency), (piece_slot_hbm, piece_slot), (tile_range_hbm, tile_range)
        ))
    ]
    late = [
        pltpu.make_async_copy(whole, held, small_sem.at[3 + n])
        for n, (whole, held) in enumerate(((eigenvalues_hbm, eigenvalues),))
    ]
    late.append(pltpu.make_async_copy(modes.at[0], my_modes, small_sem.at[4]))
    for load in routing + loads_k + late[1:]:
        load.start()

    barrier = pltpu.get_barrier_semaphore()
    for turn in range(1, slabs):
        pl.semaphore_signal(
            barrier, inc=1, device_id=(sub, lax.rem(slab + turn, slabs)), device_id_type=MESH
        )
    for turn in range(1, subs):
        pl.semaphore_signal(
            barrier, inc=1, device_id=(lax.rem(sub + turn, subs), home), device_id_type=MESH
        )

    @pl.when(home != slab)
    def _():
        pl.semaphore_signal(barrier, inc=1, device_id=(sub, home), device_id_type=MESH)

    for load in loads_m + late[:1]:
        load.start()
    for load in routing:
        load.wait()
    slots = [piece_slot[adjacency[sub, a]] for a in range(adj)]

    def owner_of(part, step):
        return part * group + lax.rem(step + sub + 1, group)

    plan = []
    for step in range(group):
        for turn in list(range(1, slabs)) + [0]:
            owner = owner_of(lax.rem(slab + turn, slabs), step)
            place = jnp.int32(0)
            for a in range(adj):
                mine = (slots[a] >= owner * owned) & (slots[a] < (owner + 1) * owned)
                place = jnp.where(mine, jnp.int32(a), place)
            start = tile_range[0, 0, place] - slab * rows
            finish = tile_range[0, 1, place] - slab * rows
            plan.append((step, turn, place, start, finish))
    row_index = lax.broadcasted_iota(jnp.int32, (rows, width), 0)
    live = {}
    for step, turn, place, start, finish in plan:
        inside = (row_index >= start) & (row_index < finish)
        live[step, turn] = inside.astype(jnp.float32).astype(jnp.bfloat16)
    for load in loads_k:
        load.wait()

    def stage(wanted, kind):
        tile = (tile_k, tile_m)[kind]
        for step, turn, place, _, _ in plan:
            if step == wanted and turn > 0:
                outgoing[step, kind, turn - 1] = tile[place] * live[step, turn]

    sends = []

    def send_columns(step, kind):
        for turn in range(1, slabs):
            part = lax.rem(slab + turn, slabs)
            copy = pltpu.make_async_remote_copy(
                src_ref=outgoing.at[step, kind, turn - 1],
                dst_ref=columns.at[step, kind, slab],
                send_sem=columns_send.at[step, kind, turn - 1],
                recv_sem=columns_recv.at[step, kind, slab],
                device_id=(sub, part),
                device_id_type=MESH,
            )
            copy.start()
            sends.append(copy)

    stage(0, 0)
    late[1].wait()
    half = rows // 2
    all_modes[slab] = jnp.concatenate([my_modes[:half], my_modes[half:]], axis=1)

    @pl.when(home != slab)
    def _():
        pl.semaphore_wait(barrier, slabs - 1 + group * slabs)

    @pl.when(home == slab)
    def _():
        pl.semaphore_wait(barrier, slabs - 1 + group * slabs - 1)

    for turn in range(1, slabs):
        part = lax.rem(slab + turn, slabs)
        copy = pltpu.make_async_remote_copy(
            src_ref=all_modes.at[slab],
            dst_ref=all_modes.at[slab],
            send_sem=modes_send.at[turn - 1],
            recv_sem=modes_recv.at[slab],
            device_id=(sub, part),
            device_id_type=MESH,
        )
        copy.start()
        sends.append(copy)
    send_columns(0, 0)
    for load in loads_m:
        load.wait()
    parts = [(step, kind) for step in range(group) for kind in range(2)]
    stage(*parts[1])
    send_columns(*parts[1])
    for part in parts[2:]:
        stage(*part)
    for step, turn, place, _, _ in plan:
        if turn == 0:
            columns[step, 0, slab] = tile_k[place] * live[step, 0]
            columns[step, 1, slab] = tile_m[place] * live[step, 0]

    takes = []
    for other in range(subs):
        theirs = [piece_slot[adjacency[other, a]] for a in range(adj)]
        takes.append([
            functools.reduce(
                lambda x, y: x | y,
                [(slot == sub * owned + q).astype(jnp.int32) for slot in theirs],
            )
            for q in range(owned)
        ])
    late[0].wait()
    eig = jnp.broadcast_to(eigenvalues[...], (width, modes.shape[2])).T
    root = lax.rsqrt(eig)

    for turn in range(1, slabs):
        part = lax.rem(slab + turn, slabs)
        pltpu.make_async_copy(all_modes.at[part], all_modes.at[part], modes_recv.at[part]).wait()
    mode_count = modes.shape[2]
    basis = jnp.concatenate([
        all_modes[part, :, side * mode_count : (side + 1) * mode_count]
        for part in range(slabs)
        for side in range(2)
    ]).T
    for step in range(group):
        owner = owner_of(slab, step)
        for kind in range(2):
            for turn in range(1, slabs):
                part = lax.rem(slab + turn, slabs)
                pltpu.make_async_copy(
                    columns.at[step, kind, part],
                    columns.at[step, kind, part],
                    columns_recv.at[step, kind, part],
                ).wait()
            following = 2 * step + kind + 2
            if following < len(parts):
                send_columns(*parts[following])
            proj = jnp.dot(
                basis,
                columns[step, kind].reshape(slabs * rows, width),
                preferred_element_type=jnp.float32,
            )
            if kind == 0:
                ratio = proj / eig
                first = (proj * root).astype(jnp.bfloat16)
                gram_part = contract_rows(first, first)
            else:
                second = (ratio - proj).astype(jnp.bfloat16)
                third = proj.astype(jnp.bfloat16)
                gram_part = contract_rows(
                    jnp.concatenate([second, third]), jnp.concatenate([second, -third])
                )
            blocks[step, kind] = gram_part.astype(jnp.bfloat16).reshape(slabs, quarter, width)
            for turn in range(1, slabs + 1):
                part = lax.rem(slab + turn, slabs)
                copy = pltpu.make_async_remote_copy(
                    src_ref=blocks.at[step, kind, part],
                    dst_ref=arrived.at[sub, kind],
                    send_sem=blocks_send.at[step, kind, turn - 1],
                    recv_sem=blocks_recv.at[sub, kind],
                    device_id=(owner, part),
                    device_id_type=MESH,
                )
                if turn < slabs:
                    copy.start()
                    sends.append(copy)
                else:
                    pl.when(owner != sub)(copy.start)

        @pl.when(owner == sub)
        def _():
            for kind in range(2):
                arrived[sub, kind] = blocks[step, kind, slab]

    for copy in sends:
        copy.wait_send()
    for step in range(group):

        @pl.when(owner_of(slab, step) != sub)
        def _():
            for kind in range(2):
                mine = blocks.at[step, kind, slab]
                pltpu.make_async_copy(mine, mine, blocks_send.at[step, kind, slabs - 1]).wait()

    total = [[jnp.zeros((quarter, width), jnp.float32)] * owned for _ in range(2)]
    for other in range(subs):

        @pl.when((other != sub) | (home != slab))
        def _():
            for kind in range(2):
                theirs = arrived.at[other, kind]
                pltpu.make_async_copy(theirs, theirs, blocks_recv.at[other, kind]).wait()

        for kind in range(2):
            term = arrived[other, kind].astype(jnp.float32)
            for q in range(owned):
                total[kind][q] = total[kind][q] + jnp.where(takes[other][q] > 0, term, 0.0)
    for q in range(owned):
        gram[0, q] = total[0][q]
        gram[1, q] = total[1][q]


def dense_body(
    subs,
    slabs,
    mode_shapes,
    coupling_k,
    coupling_m,
    tile_range,
    eigenvalues,
    adjacency,
    piece_slot,
    interface_k,
    interface_m,
):
    _, rows, mode_count = mode_shapes.shape
    adj = adjacency.shape[1]
    owned, quarter, width = interface_k.shape
    group = subs // slabs
    vmem = pl.BlockSpec(memory_space=pltpu.VMEM)
    hbm = pl.BlockSpec(memory_space=pltpu.HBM)
    gram = pl.pallas_call(
        functools.partial(kernel, subs, slabs),
        out_shape=pltpu.VMEM((2,) + interface_k.shape, jnp.float32),
        in_specs=[hbm] * 7,
        out_specs=vmem,
        scratch_shapes=[
            pltpu.SMEM(adjacency.shape, adjacency.dtype),
            pltpu.SMEM(piece_slot.shape, piece_slot.dtype),
            pltpu.SMEM(tile_range.shape, tile_range.dtype),
            pltpu.VMEM(eigenvalues.shape, eigenvalues.dtype),
            pltpu.VMEM((rows, mode_count), jnp.bfloat16),
            pltpu.VMEM((adj, rows, width), jnp.bfloat16),
            pltpu.VMEM((adj, rows, width), jnp.bfloat16),
            pltpu.VMEM((group, 2, slabs - 1, rows, width), jnp.bfloat16),
            pltpu.VMEM((group, 2, slabs, rows, width), jnp.bfloat16),
            pltpu.VMEM((slabs, rows // 2, 2 * mode_count), jnp.bfloat16),
            pltpu.VMEM((group, 2, slabs, quarter, width), jnp.bfloat16),
            pltpu.VMEM((subs, 2, quarter, width), jnp.bfloat16),
            pltpu.SemaphoreType.DMA((5,)),
            pltpu.SemaphoreType.DMA((2, adj)),
            pltpu.SemaphoreType.DMA((slabs - 1,)),
            pltpu.SemaphoreType.DMA((slabs,)),
            pltpu.SemaphoreType.DMA((group, 2, slabs - 1)),
            pltpu.SemaphoreType.DMA((group, 2, slabs)),
            pltpu.SemaphoreType.DMA((group, 2, slabs)),
            pltpu.SemaphoreType.DMA((subs, 2)),
        ],
        compiler_params=pltpu.CompilerParams(
            collective_id=0, has_side_effects=True, vmem_limit_bytes=56 * 1024 * 1024
        ),
    )(
        adjacency,
        piece_slot,
        tile_range,
        eigenvalues,
        mode_shapes,
        coupling_k,
        coupling_m,
    )
    return (interface_k + gram[0], interface_m + gram[1])


def sparse_body(
    mode_shapes,
    coupling_k,
    coupling_m,
    tile_range,
    eigenvalues,
    adjacency,
    piece_slot,
    interface_k,
    interface_m,
):
    row_count = mode_shapes.shape[1]
    mode_count = mode_shapes.shape[2]
    adj_count = adjacency.shape[1]
    piece_width = interface_k.shape[2]
    owned_count = interface_k.shape[0]
    quarter_rows = interface_k.shape[1]
    sub_count = lax.axis_size("sub")
    slab_pos = lax.axis_index("slab")
    sub_pos = lax.axis_index("sub")
    row_index = slab_pos * row_count + lax.iota(jnp.int32, row_count)
    live = (
        (row_index[:, None] >= tile_range[0, 0][None, :])
        & (row_index[:, None] < tile_range[0, 1][None, :])
    ).astype(jnp.bfloat16)
    stiff_rows = (
        coupling_k[0].reshape(row_count, adj_count, piece_width) * live[:, :, None]
    ).reshape(row_count, adj_count * piece_width)
    mass_rows = (
        coupling_m[0].reshape(row_count, adj_count, piece_width) * live[:, :, None]
    ).reshape(row_count, adj_count * piece_width)
    part_s = jnp.einsum("rm,rc->mc", mode_shapes[0], stiff_rows, preferred_element_type=jnp.float32)
    part_v = jnp.einsum("rm,rc->mc", mode_shapes[0], mass_rows, preferred_element_type=jnp.float32)
    proj_s, proj_v = lax.psum((part_s, part_v), "slab")
    eig_held = eigenvalues[0]
    eig_col = eig_held[:, None]
    first = (proj_s * lax.rsqrt(eig_col)).astype(jnp.bfloat16)
    second = (proj_s / eig_col - proj_v).astype(jnp.bfloat16)
    third = proj_v.astype(jnp.bfloat16)
    stacked = jnp.stack([first, second, third]).reshape(3, mode_count, adj_count, piece_width)
    my_slots = piece_slot[adjacency[sub_pos]]
    owner_hot = (
        my_slots[None, :] // owned_count == lax.iota(jnp.int32, sub_count)[:, None]
    ).astype(jnp.bfloat16)
    outgoing = jnp.einsum(
        "oa,kmab->okmb", owner_hot, stacked, preferred_element_type=jnp.float32
    ).astype(jnp.bfloat16)
    incoming = lax.all_to_all(outgoing, "sub", split_axis=0, concat_axis=0, tiled=True)
    all_slots = piece_slot[adjacency]
    targets = sub_pos * owned_count + lax.iota(jnp.int32, owned_count)
    select = jnp.any(all_slots[:, :, None] == targets[None, None, :], axis=1).astype(jnp.bfloat16)

    def piece_gram(weights):
        picked = incoming * weights[:, None, None, None]
        left_side = lax.dynamic_slice_in_dim(picked, slab_pos * quarter_rows, quarter_rows, 3)
        gram_stiff = jnp.einsum(
            "smb,smc->bc", left_side[:, 0], incoming[:, 0], preferred_element_type=jnp.float32
        )
        gram_mass = jnp.einsum(
            "smb,smc->bc", left_side[:, 1], incoming[:, 1], preferred_element_type=jnp.float32
        )
        gram_mass = gram_mass - jnp.einsum(
            "smb,smc->bc", left_side[:, 2], incoming[:, 2], preferred_element_type=jnp.float32
        )
        return (gram_stiff, gram_mass)

    gram_k, gram_m = lax.map(piece_gram, select.T)
    return (interface_k + gram_k, interface_m + gram_m)


def body(subs, slabs, *arrays):
    adjacency = arrays[5]
    if adjacency.shape[1] == subs and subs % slabs == 0:
        return dense_body(subs, slabs, *arrays)
    return sparse_body(*arrays)


def solution(mesh):
    placed = (
        P("sub", "slab", None),
        P("sub", "slab", None),
        P("sub", "slab", None),
        P("sub", None, None),
        P("sub", None),
        P(),
        P(),
        P("sub", "slab", None),
        P("sub", "slab", None),
    )
    return jax.shard_map(
        functools.partial(body, mesh.shape["sub"], mesh.shape["slab"]),
        mesh=mesh,
        in_specs=placed,
        out_specs=(P("sub", "slab", None), P("sub", "slab", None)),
        check_vma=False,
    )
```

```python
import functools

import jax
import jax.numpy as jnp
from jax import lax
from jax.experimental import pallas as pl
from jax.experimental.pallas import tpu as pltpu
from jax.sharding import PartitionSpec as P

MESH = pl.DeviceIdType.MESH


def contract_rows(left, right):
    return lax.dot_general(
        left, right, (((0,), (0,)), ((), ())), preferred_element_type=jnp.float32
    )


def kernel(
    subs,
    slabs,
    adjacency_hbm,
    piece_slot_hbm,
    tile_range_hbm,
    eigenvalues_hbm,
    modes,
    coupling_k,
    coupling_m,
    gram,
    adjacency,
    piece_slot,
    tile_range,
    eigenvalues,
    my_modes,
    tile_k,
    tile_m,
    outgoing,
    columns,
    all_modes,
    blocks,
    arrived,
    small_sem,
    local_sem,
    modes_send,
    modes_recv,
    columns_send,
    columns_recv,
    blocks_send,
    blocks_recv,
):
    sub = lax.axis_index("sub")
    slab = lax.axis_index("slab")
    group = subs // slabs
    adj = adjacency.shape[1]
    _, owned, quarter, width = gram.shape
    rows = modes.shape[1]
    home = lax.rem(sub, slabs)

    loads = [
        pltpu.make_async_copy(
            whole.at[0, :, a * width : (a + 1) * width], tile.at[a], local_sem.at[kind, a]
        )
        for a in range(adj)
        for kind, (whole, tile) in enumerate(((coupling_k, tile_k), (coupling_m, tile_m)))
    ]
    routing = [
        pltpu.make_async_copy(whole, held, small_sem.at[n])
        for n, (whole, held) in enumerate((
            (adjacency_hbm, adjacency), (piece_slot_hbm, piece_slot), (tile_range_hbm, tile_range)
        ))
    ]
    late = [
        pltpu.make_async_copy(whole, held, small_sem.at[3 + n])
        for n, (whole, held) in enumerate(((eigenvalues_hbm, eigenvalues),))
    ]
    late.append(pltpu.make_async_copy(modes.at[0], my_modes, small_sem.at[4]))
    for load in routing + late[1:] + loads:
        load.start()

    barrier = pltpu.get_barrier_semaphore()
    for turn in range(1, slabs):
        pl.semaphore_signal(
            barrier, inc=1, device_id=(sub, lax.rem(slab + turn, slabs)), device_id_type=MESH
        )
    for turn in range(1, subs):
        pl.semaphore_signal(
            barrier, inc=1, device_id=(lax.rem(sub + turn, subs), home), device_id_type=MESH
        )

    @pl.when(home != slab)
    def _():
        pl.semaphore_signal(barrier, inc=1, device_id=(sub, home), device_id_type=MESH)

    late[0].start()
    late[1].wait()
    half = rows // 2
    all_modes[slab] = jnp.concatenate([my_modes[:half], my_modes[half:]], axis=1)
    for load in routing:
        load.wait()
    slots = [piece_slot[adjacency[sub, a]] for a in range(adj)]

    def owner_of(part, step):
        return part + slabs * lax.rem(step + sub // slabs + 1, group)

    plan = []
    for step in range(group):
        for turn in list(range(1, slabs)) + [0]:
            owner = owner_of(lax.rem(slab + turn, slabs), step)
            place = jnp.int32(0)
            for a in range(adj):
                mine = (slots[a] >= owner * owned) & (slots[a] < (owner + 1) * owned)
                place = jnp.where(mine, jnp.int32(a), place)
            start = tile_range[0, 0, place] - slab * rows
            finish = tile_range[0, 1, place] - slab * rows
            plan.append((step, turn, place, start, finish))
    row_index = lax.broadcasted_iota(jnp.int32, (rows, width), 0)
    live = {}
    for step, turn, place, start, finish in plan:
        inside = (row_index >= start) & (row_index < finish)
        live[step, turn] = inside.astype(jnp.float32).astype(jnp.bfloat16)
    for load in loads:
        load.wait()

    def stage(wanted, kind):
        tile = (tile_k, tile_m)[kind]
        for step, turn, place, _, _ in plan:
            if step == wanted and turn > 0:
                outgoing[step, kind, turn - 1] = tile[place] * live[step, turn]

    sends = []

    def send_columns(step, kind):
        for turn in range(1, slabs):
            part = lax.rem(slab + turn, slabs)
            copy = pltpu.make_async_remote_copy(
                src_ref=outgoing.at[step, kind, turn - 1],
                dst_ref=columns.at[step, kind, slab],
                send_sem=columns_send.at[step, kind, turn - 1],
                recv_sem=columns_recv.at[step, kind, slab],
                device_id=(sub, part),
                device_id_type=MESH,
            )
            copy.start()
            sends.append(copy)

    stage(0, 0)

    @pl.when(home != slab)
    def _():
        pl.semaphore_wait(barrier, slabs - 1 + group * slabs)

    @pl.when(home == slab)
    def _():
        pl.semaphore_wait(barrier, slabs - 1 + group * slabs - 1)

    for turn in range(1, slabs):
        part = lax.rem(slab + turn, slabs)
        copy = pltpu.make_async_remote_copy(
            src_ref=all_modes.at[slab],
            dst_ref=all_modes.at[slab],
            send_sem=modes_send.at[turn - 1],
            recv_sem=modes_recv.at[slab],
            device_id=(sub, part),
            device_id_type=MESH,
        )
        copy.start()
        sends.append(copy)
    send_columns(0, 0)
    for step in range(group):
        for kind in range(2):
            if step + kind > 0:
                stage(step, kind)
                send_columns(step, kind)
    for step, turn, place, _, _ in plan:
        if turn == 0:
            columns[step, 0, slab] = tile_k[place] * live[step, 0]
            columns[step, 1, slab] = tile_m[place] * live[step, 0]

    takes = []
    for other in range(subs):
        theirs = [piece_slot[adjacency[other, a]] for a in range(adj)]
        takes.append([
            functools.reduce(
                lambda x, y: x | y,
                [(slot == sub * owned + q).astype(jnp.int32) for slot in theirs],
            )
            for q in range(owned)
        ])
    late[0].wait()
    eig = jnp.broadcast_to(eigenvalues[...], (width, modes.shape[2])).T
    root = lax.rsqrt(eig)

    for turn in range(1, slabs):
        part = lax.rem(slab + turn, slabs)
        pltpu.make_async_copy(all_modes.at[part], all_modes.at[part], modes_recv.at[part]).wait()
    mode_count = modes.shape[2]
    basis = jnp.concatenate([
        all_modes[part, :, side * mode_count : (side + 1) * mode_count]
        for part in range(slabs)
        for side in range(2)
    ]).T
    for step in range(group):
        owner = owner_of(slab, step)
        for kind in range(2):
            for turn in range(1, slabs):
                part = lax.rem(slab + turn, slabs)
                pltpu.make_async_copy(
                    columns.at[step, kind, part],
                    columns.at[step, kind, part],
                    columns_recv.at[step, kind, part],
                ).wait()
            proj = jnp.dot(
                basis,
                columns[step, kind].reshape(slabs * rows, width),
                preferred_element_type=jnp.float32,
            )
            if kind == 0:
                proj_s = proj
                first = (proj_s * root).astype(jnp.bfloat16)
                gram_part = contract_rows(first, first)
            else:
                second = (proj_s / eig - proj).astype(jnp.bfloat16)
                third = proj.astype(jnp.bfloat16)
                gram_part = contract_rows(
                    jnp.concatenate([second, third]), jnp.concatenate([second, -third])
                )
            blocks[step, kind] = gram_part.astype(jnp.bfloat16).reshape(slabs, quarter, width)
            for turn in range(1, slabs + 1):
                part = lax.rem(slab + turn, slabs)
                copy = pltpu.make_async_remote_copy(
                    src_ref=blocks.at[step, kind, part],
                    dst_ref=arrived.at[sub, kind],
                    send_sem=blocks_send.at[step, kind, turn - 1],
                    recv_sem=blocks_recv.at[sub, kind],
                    device_id=(owner, part),
                    device_id_type=MESH,
                )
                if turn < slabs:
                    copy.start()
                    sends.append(copy)
                else:
                    pl.when(owner != sub)(copy.start)

        @pl.when(owner == sub)
        def _():
            for kind in range(2):
                arrived[sub, kind] = blocks[step, kind, slab]

    for copy in sends:
        copy.wait_send()
    for step in range(group):

        @pl.when(owner_of(slab, step) != sub)
        def _():
            for kind in range(2):
                mine = blocks.at[step, kind, slab]
                pltpu.make_async_copy(mine, mine, blocks_send.at[step, kind, slabs - 1]).wait()

    total = [[jnp.zeros((quarter, width), jnp.float32)] * owned for _ in range(2)]
    for other in range(subs):

        @pl.when((other != sub) | (home != slab))
        def _():
            for kind in range(2):
                theirs = arrived.at[other, kind]
                pltpu.make_async_copy(theirs, theirs, blocks_recv.at[other, kind]).wait()

        for kind in range(2):
            term = arrived[other, kind].astype(jnp.float32)
            for q in range(owned):
                total[kind][q] = total[kind][q] + jnp.where(takes[other][q] > 0, term, 0.0)
    for q in range(owned):
        gram[0, q] = total[0][q]
        gram[1, q] = total[1][q]


def dense_body(
    subs,
    slabs,
    mode_shapes,
    coupling_k,
    coupling_m,
    tile_range,
    eigenvalues,
    adjacency,
    piece_slot,
    interface_k,
    interface_m,
):
    _, rows, mode_count = mode_shapes.shape
    adj = adjacency.shape[1]
    owned, quarter, width = interface_k.shape
    group = subs // slabs
    vmem = pl.BlockSpec(memory_space=pltpu.VMEM)
    hbm = pl.BlockSpec(memory_space=pltpu.HBM)
    gram = pl.pallas_call(
        functools.partial(kernel, subs, slabs),
        out_shape=pltpu.VMEM((2,) + interface_k.shape, jnp.float32),
        in_specs=[hbm] * 7,
        out_specs=vmem,
        scratch_shapes=[
            pltpu.SMEM(adjacency.shape, adjacency.dtype),
            pltpu.SMEM(piece_slot.shape, piece_slot.dtype),
            pltpu.SMEM(tile_range.shape, tile_range.dtype),
            pltpu.VMEM(eigenvalues.shape, eigenvalues.dtype),
            pltpu.VMEM((rows, mode_count), jnp.bfloat16),
            pltpu.VMEM((adj, rows, width), jnp.bfloat16),
            pltpu.VMEM((adj, rows, width), jnp.bfloat16),
            pltpu.VMEM((group, 2, slabs - 1, rows, width), jnp.bfloat16),
            pltpu.VMEM((group, 2, slabs, rows, width), jnp.bfloat16),
            pltpu.VMEM((slabs, rows // 2, 2 * mode_count), jnp.bfloat16),
            pltpu.VMEM((group, 2, slabs, quarter, width), jnp.bfloat16),
            pltpu.VMEM((subs, 2, quarter, width), jnp.bfloat16),
            pltpu.SemaphoreType.DMA((5,)),
            pltpu.SemaphoreType.DMA((2, adj)),
            pltpu.SemaphoreType.DMA((slabs - 1,)),
            pltpu.SemaphoreType.DMA((slabs,)),
            pltpu.SemaphoreType.DMA((group, 2, slabs - 1)),
            pltpu.SemaphoreType.DMA((group, 2, slabs)),
            pltpu.SemaphoreType.DMA((group, 2, slabs)),
            pltpu.SemaphoreType.DMA((subs, 2)),
        ],
        compiler_params=pltpu.CompilerParams(
            collective_id=0, has_side_effects=True, vmem_limit_bytes=56 * 1024 * 1024
        ),
    )(
        adjacency,
        piece_slot,
        tile_range,
        eigenvalues,
        mode_shapes,
        coupling_k,
        coupling_m,
    )
    return (interface_k + gram[0], interface_m + gram[1])


def sparse_body(
    mode_shapes,
    coupling_k,
    coupling_m,
    tile_range,
    eigenvalues,
    adjacency,
    piece_slot,
    interface_k,
    interface_m,
):
    row_count = mode_shapes.shape[1]
    mode_count = mode_shapes.shape[2]
    adj_count = adjacency.shape[1]
    piece_width = interface_k.shape[2]
    owned_count = interface_k.shape[0]
    quarter_rows = interface_k.shape[1]
    sub_count = lax.axis_size("sub")
    slab_pos = lax.axis_index("slab")
    sub_pos = lax.axis_index("sub")
    row_index = slab_pos * row_count + lax.iota(jnp.int32, row_count)
    live = (
        (row_index[:, None] >= tile_range[0, 0][None, :])
        & (row_index[:, None] < tile_range[0, 1][None, :])
    ).astype(jnp.bfloat16)
    stiff_rows = (
        coupling_k[0].reshape(row_count, adj_count, piece_width) * live[:, :, None]
    ).reshape(row_count, adj_count * piece_width)
    mass_rows = (
        coupling_m[0].reshape(row_count, adj_count, piece_width) * live[:, :, None]
    ).reshape(row_count, adj_count * piece_width)
    part_s = jnp.einsum("rm,rc->mc", mode_shapes[0], stiff_rows, preferred_element_type=jnp.float32)
    part_v = jnp.einsum("rm,rc->mc", mode_shapes[0], mass_rows, preferred_element_type=jnp.float32)
    proj_s, proj_v = lax.psum((part_s, part_v), "slab")
    eig_held = eigenvalues[0]
    eig_col = eig_held[:, None]
    first = (proj_s * lax.rsqrt(eig_col)).astype(jnp.bfloat16)
    second = (proj_s / eig_col - proj_v).astype(jnp.bfloat16)
    third = proj_v.astype(jnp.bfloat16)
    stacked = jnp.stack([first, second, third]).reshape(3, mode_count, adj_count, piece_width)
    my_slots = piece_slot[adjacency[sub_pos]]
    owner_hot = (
        my_slots[None, :] // owned_count == lax.iota(jnp.int32, sub_count)[:, None]
    ).astype(jnp.bfloat16)
    outgoing = jnp.einsum(
        "oa,kmab->okmb", owner_hot, stacked, preferred_element_type=jnp.float32
    ).astype(jnp.bfloat16)
    incoming = lax.all_to_all(outgoing, "sub", split_axis=0, concat_axis=0, tiled=True)
    all_slots = piece_slot[adjacency]
    targets = sub_pos * owned_count + lax.iota(jnp.int32, owned_count)
    select = jnp.any(all_slots[:, :, None] == targets[None, None, :], axis=1).astype(jnp.bfloat16)

    def piece_gram(weights):
        picked = incoming * weights[:, None, None, None]
        left_side = lax.dynamic_slice_in_dim(picked, slab_pos * quarter_rows, quarter_rows, 3)
        gram_stiff = jnp.einsum(
            "smb,smc->bc", left_side[:, 0], incoming[:, 0], preferred_element_type=jnp.float32
        )
        gram_mass = jnp.einsum(
            "smb,smc->bc", left_side[:, 1], incoming[:, 1], preferred_element_type=jnp.float32
        )
        gram_mass = gram_mass - jnp.einsum(
            "smb,smc->bc", left_side[:, 2], incoming[:, 2], preferred_element_type=jnp.float32
        )
        return (gram_stiff, gram_mass)

    gram_k, gram_m = lax.map(piece_gram, select.T)
    return (interface_k + gram_k, interface_m + gram_m)


def body(subs, slabs, *arrays):
    adjacency = arrays[5]
    if adjacency.shape[1] == subs and subs % slabs == 0:
        return dense_body(subs, slabs, *arrays)
    return sparse_body(*arrays)


def solution(mesh):
    placed = (
        P("sub", "slab", None),
        P("sub", "slab", None),
        P("sub", "slab", None),
        P("sub", None, None),
        P("sub", None),
        P(),
        P(),
        P("sub", "slab", None),
        P("sub", "slab", None),
    )
    return jax.shard_map(
        functools.partial(body, mesh.shape["sub"], mesh.shape["slab"]),
        mesh=mesh,
        in_specs=placed,
        out_specs=(P("sub", "slab", None), P("sub", "slab", None)),
        check_vma=False,
    )
```

```python
import functools

import jax
import jax.numpy as jnp
from jax import lax
from jax.experimental import pallas as pl
from jax.experimental.pallas import tpu as pltpu
from jax.sharding import PartitionSpec as P

MESH = pl.DeviceIdType.MESH


def contract_rows(left, right):
    return lax.dot_general(
        left, right, (((0,), (0,)), ((), ())), preferred_element_type=jnp.float32
    )


def kernel(
    subs,
    slabs,
    adjacency_hbm,
    piece_slot_hbm,
    tile_range_hbm,
    eigenvalues_hbm,
    modes,
    coupling_k,
    coupling_m,
    gram,
    adjacency,
    piece_slot,
    tile_range,
    eigenvalues,
    adjacency_rows,
    my_modes,
    tile_k,
    tile_m,
    outgoing,
    columns,
    all_modes,
    blocks,
    arrived,
    small_sem,
    local_sem,
    modes_send,
    modes_recv,
    columns_send,
    columns_recv,
    blocks_send,
    blocks_recv,
):
    sub = lax.axis_index("sub")
    slab = lax.axis_index("slab")
    group = subs // slabs
    adj = adjacency.shape[1]
    _, owned, quarter, width = gram.shape
    rows = modes.shape[1]
    home = lax.rem(sub, slabs)

    loads = [
        pltpu.make_async_copy(
            whole.at[0, :, a * width : (a + 1) * width], tile.at[a], local_sem.at[kind, a]
        )
        for a in range(adj)
        for kind, (whole, tile) in enumerate(((coupling_k, tile_k), (coupling_m, tile_m)))
    ]
    routing = [
        pltpu.make_async_copy(whole, held, small_sem.at[n])
        for n, (whole, held) in enumerate((
            (adjacency_hbm, adjacency), (piece_slot_hbm, piece_slot), (tile_range_hbm, tile_range)
        ))
    ]
    late = [
        pltpu.make_async_copy(whole, held, small_sem.at[3 + n])
        for n, (whole, held) in enumerate(((eigenvalues_hbm, eigenvalues),))
    ]
    late.append(pltpu.make_async_copy(modes.at[0], my_modes, small_sem.at[4]))
    late.append(pltpu.make_async_copy(adjacency_hbm, adjacency_rows, small_sem.at[5]))
    for load in routing + late[1:2] + loads:
        load.start()

    barrier = pltpu.get_barrier_semaphore()
    for turn in range(1, slabs):
        pl.semaphore_signal(
            barrier, inc=1, device_id=(sub, lax.rem(slab + turn, slabs)), device_id_type=MESH
        )
    for turn in range(1, subs):
        pl.semaphore_signal(
            barrier, inc=1, device_id=(lax.rem(sub + turn, subs), home), device_id_type=MESH
        )

    @pl.when(home != slab)
    def _():
        pl.semaphore_signal(barrier, inc=1, device_id=(sub, home), device_id_type=MESH)

    late[0].start()
    late[2].start()
    late[1].wait()
    half = rows // 2
    all_modes[slab] = jnp.concatenate([my_modes[:half], my_modes[half:]], axis=1)
    for load in routing:
        load.wait()
    slots = [piece_slot[adjacency[sub, a]] for a in range(adj)]

    def owner_of(part, step):
        return part + slabs * lax.rem(step + sub // slabs + 1, group)

    plan = []
    for step in range(group):
        for turn in list(range(1, slabs)) + [0]:
            owner = owner_of(lax.rem(slab + turn, slabs), step)
            place = jnp.int32(0)
            for a in range(adj):
                mine = (slots[a] >= owner * owned) & (slots[a] < (owner + 1) * owned)
                place = jnp.where(mine, jnp.int32(a), place)
            start = tile_range[0, 0, place] - slab * rows
            finish = tile_range[0, 1, place] - slab * rows
            plan.append((step, turn, place, start, finish))
    row_index = lax.broadcasted_iota(jnp.int32, (rows, width), 0)
    live = {}
    for step, turn, place, start, finish in plan:
        inside = (row_index >= start) & (row_index < finish)
        live[step, turn] = inside.astype(jnp.float32).astype(jnp.bfloat16)
    for load in loads:
        load.wait()

    def stage(wanted, kind):
        tile = (tile_k, tile_m)[kind]
        for step, turn, place, _, _ in plan:
            if step == wanted and turn > 0:
                outgoing[step, kind, turn - 1] = tile[place] * live[step, turn]

    sends = []

    def send_columns(step, kind):
        for turn in range(1, slabs):
            part = lax.rem(slab + turn, slabs)
            copy = pltpu.make_async_remote_copy(
                src_ref=outgoing.at[step, kind, turn - 1],
                dst_ref=columns.at[step, kind, slab],
                send_sem=columns_send.at[step, kind, turn - 1],
                recv_sem=columns_recv.at[step, kind, slab],
                device_id=(sub, part),
                device_id_type=MESH,
            )
            copy.start()
            sends.append(copy)

    stage(0, 0)

    @pl.when(home != slab)
    def _():
        pl.semaphore_wait(barrier, slabs - 1 + group * slabs)

    @pl.when(home == slab)
    def _():
        pl.semaphore_wait(barrier, slabs - 1 + group * slabs - 1)

    for turn in range(1, slabs):
        part = lax.rem(slab + turn, slabs)
        copy = pltpu.make_async_remote_copy(
            src_ref=all_modes.at[slab],
            dst_ref=all_modes.at[slab],
            send_sem=modes_send.at[turn - 1],
            recv_sem=modes_recv.at[slab],
            device_id=(sub, part),
            device_id_type=MESH,
        )
        copy.start()
        sends.append(copy)
    send_columns(0, 0)
    for step in range(group):
        for kind in range(2):
            if step + kind > 0:
                stage(step, kind)
                send_columns(step, kind)
    for step, turn, place, _, _ in plan:
        if turn == 0:
            columns[step, 0, slab] = tile_k[place] * live[step, 0]
            columns[step, 1, slab] = tile_m[place] * live[step, 0]

    late[2].wait()
    takes = []
    for q in range(owned):
        piece = jnp.int32(0)
        for p in range(piece_slot.shape[0]):
            piece = jnp.where(piece_slot[p] == sub * owned + q, jnp.int32(p), piece)
        hits = (adjacency_rows[...] == piece).astype(jnp.float32)
        takes.append(jnp.max(hits, axis=1, keepdims=True))
    late[0].wait()
    eig = jnp.broadcast_to(eigenvalues[...], (width, modes.shape[2])).T
    root = lax.rsqrt(eig)

    for turn in range(1, slabs):
        part = lax.rem(slab + turn, slabs)
        pltpu.make_async_copy(all_modes.at[part], all_modes.at[part], modes_recv.at[part]).wait()
    mode_count = modes.shape[2]
    basis = jnp.concatenate([
        all_modes[part, :, side * mode_count : (side + 1) * mode_count]
        for part in range(slabs)
        for side in range(2)
    ]).T
    for step in range(group):
        owner = owner_of(slab, step)
        for kind in range(2):
            for turn in range(1, slabs):
                part = lax.rem(slab + turn, slabs)
                pltpu.make_async_copy(
                    columns.at[step, kind, part],
                    columns.at[step, kind, part],
                    columns_recv.at[step, kind, part],
                ).wait()
            proj = jnp.dot(
                basis,
                columns[step, kind].reshape(slabs * rows, width),
                preferred_element_type=jnp.float32,
            )
            if kind == 0:
                proj_s = proj
                first = (proj_s * root).astype(jnp.bfloat16)
                gram_part = contract_rows(first, first)
            else:
                second = (proj_s / eig - proj).astype(jnp.bfloat16)
                third = proj.astype(jnp.bfloat16)
                gram_part = contract_rows(
                    jnp.concatenate([second, third]), jnp.concatenate([second, -third])
                )
            blocks[step, kind] = gram_part.astype(jnp.bfloat16).reshape(slabs, quarter, width)
            for turn in range(1, slabs + 1):
                part = lax.rem(slab + turn, slabs)
                copy = pltpu.make_async_remote_copy(
                    src_ref=blocks.at[step, kind, part],
                    dst_ref=arrived.at[sub, kind],
                    send_sem=blocks_send.at[step, kind, turn - 1],
                    recv_sem=blocks_recv.at[sub, kind],
                    device_id=(owner, part),
                    device_id_type=MESH,
                )
                if turn < slabs:
                    copy.start()
                    sends.append(copy)
                else:
                    pl.when(owner != sub)(copy.start)

        @pl.when(owner == sub)
        def _():
            for kind in range(2):
                arrived[sub, kind] = blocks[step, kind, slab]

    for copy in sends:
        copy.wait_send()
    for step in range(group):

        @pl.when(owner_of(slab, step) != sub)
        def _():
            for kind in range(2):
                mine = blocks.at[step, kind, slab]
                pltpu.make_async_copy(mine, mine, blocks_send.at[step, kind, slabs - 1]).wait()

    total = [[jnp.zeros((quarter, width), jnp.float32)] * owned for _ in range(2)]
    for other in range(subs):

        @pl.when((other != sub) | (home != slab))
        def _():
            for kind in range(2):
                theirs = arrived.at[other, kind]
                pltpu.make_async_copy(theirs, theirs, blocks_recv.at[other, kind]).wait()

        taken = [
            jnp.broadcast_to(takes[q][other : other + 1], (quarter, width)) > 0
            for q in range(owned)
        ]
        for kind in range(2):
            term = arrived[other, kind].astype(jnp.float32)
            for q in range(owned):
                total[kind][q] = total[kind][q] + jnp.where(taken[q], term, 0.0)
    for q in range(owned):
        gram[0, q] = total[0][q]
        gram[1, q] = total[1][q]


def dense_body(
    subs,
    slabs,
    mode_shapes,
    coupling_k,
    coupling_m,
    tile_range,
    eigenvalues,
    adjacency,
    piece_slot,
    interface_k,
    interface_m,
):
    _, rows, mode_count = mode_shapes.shape
    adj = adjacency.shape[1]
    owned, quarter, width = interface_k.shape
    group = subs // slabs
    vmem = pl.BlockSpec(memory_space=pltpu.VMEM)
    hbm = pl.BlockSpec(memory_space=pltpu.HBM)
    gram = pl.pallas_call(
        functools.partial(kernel, subs, slabs),
        out_shape=pltpu.VMEM((2,) + interface_k.shape, jnp.float32),
        in_specs=[hbm] * 7,
        out_specs=vmem,
        scratch_shapes=[
            pltpu.SMEM(adjacency.shape, adjacency.dtype),
            pltpu.SMEM(piece_slot.shape, piece_slot.dtype),
            pltpu.SMEM(tile_range.shape, tile_range.dtype),
            pltpu.VMEM(eigenvalues.shape, eigenvalues.dtype),
            pltpu.VMEM(adjacency.shape, adjacency.dtype),
            pltpu.VMEM((rows, mode_count), jnp.bfloat16),
            pltpu.VMEM((adj, rows, width), jnp.bfloat16),
            pltpu.VMEM((adj, rows, width), jnp.bfloat16),
            pltpu.VMEM((group, 2, slabs - 1, rows, width), jnp.bfloat16),
            pltpu.VMEM((group, 2, slabs, rows, width), jnp.bfloat16),
            pltpu.VMEM((slabs, rows // 2, 2 * mode_count), jnp.bfloat16),
            pltpu.VMEM((group, 2, slabs, quarter, width), jnp.bfloat16),
            pltpu.VMEM((subs, 2, quarter, width), jnp.bfloat16),
            pltpu.SemaphoreType.DMA((6,)),
            pltpu.SemaphoreType.DMA((2, adj)),
            pltpu.SemaphoreType.DMA((slabs - 1,)),
            pltpu.SemaphoreType.DMA((slabs,)),
            pltpu.SemaphoreType.DMA((group, 2, slabs - 1)),
            pltpu.SemaphoreType.DMA((group, 2, slabs)),
            pltpu.SemaphoreType.DMA((group, 2, slabs)),
            pltpu.SemaphoreType.DMA((subs, 2)),
        ],
        compiler_params=pltpu.CompilerParams(
            collective_id=0, has_side_effects=True, vmem_limit_bytes=56 * 1024 * 1024
        ),
    )(
        adjacency,
        piece_slot,
        tile_range,
        eigenvalues,
        mode_shapes,
        coupling_k,
        coupling_m,
    )
    return (interface_k + gram[0], interface_m + gram[1])


def sparse_body(
    mode_shapes,
    coupling_k,
    coupling_m,
    tile_range,
    eigenvalues,
    adjacency,
    piece_slot,
    interface_k,
    interface_m,
):
    row_count = mode_shapes.shape[1]
    mode_count = mode_shapes.shape[2]
    adj_count = adjacency.shape[1]
    piece_width = interface_k.shape[2]
    owned_count = interface_k.shape[0]
    quarter_rows = interface_k.shape[1]
    sub_count = lax.axis_size("sub")
    slab_pos = lax.axis_index("slab")
    sub_pos = lax.axis_index("sub")
    row_index = slab_pos * row_count + lax.iota(jnp.int32, row_count)
    live = (
        (row_index[:, None] >= tile_range[0, 0][None, :])
        & (row_index[:, None] < tile_range[0, 1][None, :])
    ).astype(jnp.bfloat16)
    stiff_rows = (
        coupling_k[0].reshape(row_count, adj_count, piece_width) * live[:, :, None]
    ).reshape(row_count, adj_count * piece_width)
    mass_rows = (
        coupling_m[0].reshape(row_count, adj_count, piece_width) * live[:, :, None]
    ).reshape(row_count, adj_count * piece_width)
    part_s = jnp.einsum("rm,rc->mc", mode_shapes[0], stiff_rows, preferred_element_type=jnp.float32)
    part_v = jnp.einsum("rm,rc->mc", mode_shapes[0], mass_rows, preferred_element_type=jnp.float32)
    proj_s, proj_v = lax.psum((part_s, part_v), "slab")
    eig_held = eigenvalues[0]
    eig_col = eig_held[:, None]
    first = (proj_s * lax.rsqrt(eig_col)).astype(jnp.bfloat16)
    second = (proj_s / eig_col - proj_v).astype(jnp.bfloat16)
    third = proj_v.astype(jnp.bfloat16)
    stacked = jnp.stack([first, second, third]).reshape(3, mode_count, adj_count, piece_width)
    my_slots = piece_slot[adjacency[sub_pos]]
    owner_hot = (
        my_slots[None, :] // owned_count == lax.iota(jnp.int32, sub_count)[:, None]
    ).astype(jnp.bfloat16)
    outgoing = jnp.einsum(
        "oa,kmab->okmb", owner_hot, stacked, preferred_element_type=jnp.float32
    ).astype(jnp.bfloat16)
    incoming = lax.all_to_all(outgoing, "sub", split_axis=0, concat_axis=0, tiled=True)
    all_slots = piece_slot[adjacency]
    targets = sub_pos * owned_count + lax.iota(jnp.int32, owned_count)
    select = jnp.any(all_slots[:, :, None] == targets[None, None, :], axis=1).astype(jnp.bfloat16)

    def piece_gram(weights):
        picked = incoming * weights[:, None, None, None]
        left_side = lax.dynamic_slice_in_dim(picked, slab_pos * quarter_rows, quarter_rows, 3)
        gram_stiff = jnp.einsum(
            "smb,smc->bc", left_side[:, 0], incoming[:, 0], preferred_element_type=jnp.float32
        )
        gram_mass = jnp.einsum(
            "smb,smc->bc", left_side[:, 1], incoming[:, 1], preferred_element_type=jnp.float32
        )
        gram_mass = gram_mass - jnp.einsum(
            "smb,smc->bc", left_side[:, 2], incoming[:, 2], preferred_element_type=jnp.float32
        )
        return (gram_stiff, gram_mass)

    gram_k, gram_m = lax.map(piece_gram, select.T)
    return (interface_k + gram_k, interface_m + gram_m)


def body(subs, slabs, *arrays):
    adjacency = arrays[5]
    if adjacency.shape[1] == subs and subs % slabs == 0:
        return dense_body(subs, slabs, *arrays)
    return sparse_body(*arrays)


def solution(mesh):
    placed = (
        P("sub", "slab", None),
        P("sub", "slab", None),
        P("sub", "slab", None),
        P("sub", None, None),
        P("sub", None),
        P(),
        P(),
        P("sub", "slab", None),
        P("sub", "slab", None),
    )
    return jax.shard_map(
        functools.partial(body, mesh.shape["sub"], mesh.shape["slab"]),
        mesh=mesh,
        in_specs=placed,
        out_specs=(P("sub", "slab", None), P("sub", "slab", None)),
        check_vma=False,
    )
```

```python
import functools

import jax
import jax.numpy as jnp
from jax import lax
from jax.experimental import pallas as pl
from jax.experimental.pallas import tpu as pltpu
from jax.sharding import PartitionSpec as P

MESH = pl.DeviceIdType.MESH


def contract_rows(left, right):
    return lax.dot_general(
        left, right, (((0,), (0,)), ((), ())), preferred_element_type=jnp.float32
    )


def kernel(
    subs,
    slabs,
    adjacency_hbm,
    piece_slot_hbm,
    tile_range_hbm,
    eigenvalues_hbm,
    modes,
    coupling_k,
    coupling_m,
    gram,
    adjacency,
    piece_slot,
    tile_range,
    eigenvalues,
    my_modes,
    tile_k,
    tile_m,
    outgoing,
    columns,
    all_modes,
    blocks,
    arrived,
    small_sem,
    local_sem,
    modes_send,
    modes_recv,
    columns_send,
    columns_recv,
    blocks_send,
    blocks_recv,
):
    sub = lax.axis_index("sub")
    slab = lax.axis_index("slab")
    group = subs // slabs
    adj = adjacency.shape[1]
    _, owned, quarter, width = gram.shape
    rows = modes.shape[1]
    home = lax.rem(sub, slabs)

    loads = [
        pltpu.make_async_copy(
            whole.at[0, :, a * width : (a + 1) * width], tile.at[a], local_sem.at[kind, a]
        )
        for a in range(adj)
        for kind, (whole, tile) in enumerate(((coupling_k, tile_k), (coupling_m, tile_m)))
    ]
    routing = [
        pltpu.make_async_copy(whole, held, small_sem.at[n])
        for n, (whole, held) in enumerate((
            (adjacency_hbm, adjacency), (piece_slot_hbm, piece_slot), (tile_range_hbm, tile_range)
        ))
    ]
    late = [
        pltpu.make_async_copy(whole, held, small_sem.at[3 + n])
        for n, (whole, held) in enumerate(((eigenvalues_hbm, eigenvalues),))
    ]
    late.append(pltpu.make_async_copy(modes.at[0], my_modes, small_sem.at[4]))
    for load in routing + late[1:] + loads:
        load.start()

    barrier = pltpu.get_barrier_semaphore()
    for turn in range(1, slabs):
        pl.semaphore_signal(
            barrier, inc=1, device_id=(sub, lax.rem(slab + turn, slabs)), device_id_type=MESH
        )
    for turn in range(1, subs):
        pl.semaphore_signal(
            barrier, inc=1, device_id=(lax.rem(sub + turn, subs), home), device_id_type=MESH
        )

    @pl.when(home != slab)
    def _():
        pl.semaphore_signal(barrier, inc=1, device_id=(sub, home), device_id_type=MESH)

    late[0].start()
    late[1].wait()
    half = rows // 2
    all_modes[slab] = jnp.concatenate([my_modes[:half], my_modes[half:]], axis=1)
    for load in routing:
        load.wait()
    slots = [piece_slot[adjacency[sub, a]] for a in range(adj)]

    far_first = sorted(range(1, slabs), key=lambda turn: abs(slabs - 2 * turn))

    def owner_of(part, step):
        return part + slabs * lax.rem(step + sub // slabs + 1, group)

    plan = []
    for step in range(group):
        for turn in list(range(1, slabs)) + [0]:
            owner = owner_of(lax.rem(slab + turn, slabs), step)
            place = jnp.int32(0)
            for a in range(adj):
                mine = (slots[a] >= owner * owned) & (slots[a] < (owner + 1) * owned)
                place = jnp.where(mine, jnp.int32(a), place)
            start = tile_range[0, 0, place] - slab * rows
            finish = tile_range[0, 1, place] - slab * rows
            plan.append((step, turn, place, start, finish))
    row_index = lax.broadcasted_iota(jnp.int32, (rows, width), 0)
    live = {}
    for step, turn, place, start, finish in plan:
        inside = (row_index >= start) & (row_index < finish)
        live[step, turn] = inside.astype(jnp.float32).astype(jnp.bfloat16)
    for load in loads:
        load.wait()

    def stage(wanted, kind):
        tile = (tile_k, tile_m)[kind]
        for step, turn, place, _, _ in plan:
            if step == wanted and turn > 0:
                outgoing[step, kind, turn - 1] = tile[place] * live[step, turn]

    sends = []

    def send_columns(step, kind):
        for turn in far_first:
            part = lax.rem(slab + turn, slabs)
            copy = pltpu.make_async_remote_copy(
                src_ref=outgoing.at[step, kind, turn - 1],
                dst_ref=columns.at[step, kind, slab],
                send_sem=columns_send.at[step, kind, turn - 1],
                recv_sem=columns_recv.at[step, kind, slab],
                device_id=(sub, part),
                device_id_type=MESH,
            )
            copy.start()
            sends.append(copy)

    stage(0, 0)

    @pl.when(home != slab)
    def _():
        pl.semaphore_wait(barrier, slabs - 1 + group * slabs)

    @pl.when(home == slab)
    def _():
        pl.semaphore_wait(barrier, slabs - 1 + group * slabs - 1)

    for turn in far_first:
        part = lax.rem(slab + turn, slabs)
        copy = pltpu.make_async_remote_copy(
            src_ref=all_modes.at[slab],
            dst_ref=all_modes.at[slab],
            send_sem=modes_send.at[turn - 1],
            recv_sem=modes_recv.at[slab],
            device_id=(sub, part),
            device_id_type=MESH,
        )
        copy.start()
        sends.append(copy)
    send_columns(0, 0)
    for step in range(group):
        for kind in range(2):
            if step + kind > 0:
                stage(step, kind)
                send_columns(step, kind)
    for step, turn, place, _, _ in plan:
        if turn == 0:
            columns[step, 0, slab] = tile_k[place] * live[step, 0]
            columns[step, 1, slab] = tile_m[place] * live[step, 0]

    takes = []
    for other in range(subs):
        theirs = [piece_slot[adjacency[other, a]] for a in range(adj)]
        takes.append([
            functools.reduce(
                lambda x, y: x | y,
                [(slot == sub * owned + q).astype(jnp.int32) for slot in theirs],
            )
            for q in range(owned)
        ])
    late[0].wait()
    eig = jnp.broadcast_to(eigenvalues[...], (width, modes.shape[2])).T
    root = lax.rsqrt(eig)

    for turn in range(1, slabs):
        part = lax.rem(slab + turn, slabs)
        pltpu.make_async_copy(all_modes.at[part], all_modes.at[part], modes_recv.at[part]).wait()
    mode_count = modes.shape[2]
    basis = jnp.concatenate([
        all_modes[part, :, side * mode_count : (side + 1) * mode_count]
        for part in range(slabs)
        for side in range(2)
    ]).T
    for step in range(group):
        owner = owner_of(slab, step)
        for kind in range(2):
            for turn in range(1, slabs):
                part = lax.rem(slab + turn, slabs)
                pltpu.make_async_copy(
                    columns.at[step, kind, part],
                    columns.at[step, kind, part],
                    columns_recv.at[step, kind, part],
                ).wait()
            proj = jnp.dot(
                basis,
                columns[step, kind].reshape(slabs * rows, width),
                preferred_element_type=jnp.float32,
            )
            if kind == 0:
                proj_s = proj
                first = (proj_s * root).astype(jnp.bfloat16)
                gram_part = contract_rows(first, first)
            else:
                second = (proj_s / eig - proj).astype(jnp.bfloat16)
                third = proj.astype(jnp.bfloat16)
                gram_part = contract_rows(
                    jnp.concatenate([second, third]), jnp.concatenate([second, -third])
                )
            blocks[step, kind] = gram_part.astype(jnp.bfloat16).reshape(slabs, quarter, width)
            for turn in far_first + [slabs]:
                part = lax.rem(slab + turn, slabs)
                copy = pltpu.make_async_remote_copy(
                    src_ref=blocks.at[step, kind, part],
                    dst_ref=arrived.at[sub, kind],
                    send_sem=blocks_send.at[step, kind, turn - 1],
                    recv_sem=blocks_recv.at[sub, kind],
                    device_id=(owner, part),
                    device_id_type=MESH,
                )
                if turn < slabs:
                    copy.start()
                    sends.append(copy)
                else:
                    pl.when(owner != sub)(copy.start)

        @pl.when(owner == sub)
        def _():
            for kind in range(2):
                arrived[sub, kind] = blocks[step, kind, slab]

    for copy in sends:
        copy.wait_send()
    for step in range(group):

        @pl.when(owner_of(slab, step) != sub)
        def _():
            for kind in range(2):
                mine = blocks.at[step, kind, slab]
                pltpu.make_async_copy(mine, mine, blocks_send.at[step, kind, slabs - 1]).wait()

    total = [[jnp.zeros((quarter, width), jnp.float32)] * owned for _ in range(2)]
    for other in range(subs):

        @pl.when((other != sub) | (home != slab))
        def _():
            for kind in range(2):
                theirs = arrived.at[other, kind]
                pltpu.make_async_copy(theirs, theirs, blocks_recv.at[other, kind]).wait()

        for kind in range(2):
            term = arrived[other, kind].astype(jnp.float32)
            for q in range(owned):
                total[kind][q] = total[kind][q] + jnp.where(takes[other][q] > 0, term, 0.0)
    for q in range(owned):
        gram[0, q] = total[0][q]
        gram[1, q] = total[1][q]


def dense_body(
    subs,
    slabs,
    mode_shapes,
    coupling_k,
    coupling_m,
    tile_range,
    eigenvalues,
    adjacency,
    piece_slot,
    interface_k,
    interface_m,
):
    _, rows, mode_count = mode_shapes.shape
    adj = adjacency.shape[1]
    owned, quarter, width = interface_k.shape
    group = subs // slabs
    vmem = pl.BlockSpec(memory_space=pltpu.VMEM)
    hbm = pl.BlockSpec(memory_space=pltpu.HBM)
    gram = pl.pallas_call(
        functools.partial(kernel, subs, slabs),
        out_shape=pltpu.VMEM((2,) + interface_k.shape, jnp.float32),
        in_specs=[hbm] * 7,
        out_specs=vmem,
        scratch_shapes=[
            pltpu.SMEM(adjacency.shape, adjacency.dtype),
            pltpu.SMEM(piece_slot.shape, piece_slot.dtype),
            pltpu.SMEM(tile_range.shape, tile_range.dtype),
            pltpu.VMEM(eigenvalues.shape, eigenvalues.dtype),
            pltpu.VMEM((rows, mode_count), jnp.bfloat16),
            pltpu.VMEM((adj, rows, width), jnp.bfloat16),
            pltpu.VMEM((adj, rows, width), jnp.bfloat16),
            pltpu.VMEM((group, 2, slabs - 1, rows, width), jnp.bfloat16),
            pltpu.VMEM((group, 2, slabs, rows, width), jnp.bfloat16),
            pltpu.VMEM((slabs, rows // 2, 2 * mode_count), jnp.bfloat16),
            pltpu.VMEM((group, 2, slabs, quarter, width), jnp.bfloat16),
            pltpu.VMEM((subs, 2, quarter, width), jnp.bfloat16),
            pltpu.SemaphoreType.DMA((5,)),
            pltpu.SemaphoreType.DMA((2, adj)),
            pltpu.SemaphoreType.DMA((slabs - 1,)),
            pltpu.SemaphoreType.DMA((slabs,)),
            pltpu.SemaphoreType.DMA((group, 2, slabs - 1)),
            pltpu.SemaphoreType.DMA((group, 2, slabs)),
            pltpu.SemaphoreType.DMA((group, 2, slabs)),
            pltpu.SemaphoreType.DMA((subs, 2)),
        ],
        compiler_params=pltpu.CompilerParams(
            collective_id=0, has_side_effects=True, vmem_limit_bytes=56 * 1024 * 1024
        ),
    )(
        adjacency,
        piece_slot,
        tile_range,
        eigenvalues,
        mode_shapes,
        coupling_k,
        coupling_m,
    )
    return (interface_k + gram[0], interface_m + gram[1])


def sparse_body(
    mode_shapes,
    coupling_k,
    coupling_m,
    tile_range,
    eigenvalues,
    adjacency,
    piece_slot,
    interface_k,
    interface_m,
):
    row_count = mode_shapes.shape[1]
    mode_count = mode_shapes.shape[2]
    adj_count = adjacency.shape[1]
    piece_width = interface_k.shape[2]
    owned_count = interface_k.shape[0]
    quarter_rows = interface_k.shape[1]
    sub_count = lax.axis_size("sub")
    slab_pos = lax.axis_index("slab")
    sub_pos = lax.axis_index("sub")
    row_index = slab_pos * row_count + lax.iota(jnp.int32, row_count)
    live = (
        (row_index[:, None] >= tile_range[0, 0][None, :])
        & (row_index[:, None] < tile_range[0, 1][None, :])
    ).astype(jnp.bfloat16)
    stiff_rows = (
        coupling_k[0].reshape(row_count, adj_count, piece_width) * live[:, :, None]
    ).reshape(row_count, adj_count * piece_width)
    mass_rows = (
        coupling_m[0].reshape(row_count, adj_count, piece_width) * live[:, :, None]
    ).reshape(row_count, adj_count * piece_width)
    part_s = jnp.einsum("rm,rc->mc", mode_shapes[0], stiff_rows, preferred_element_type=jnp.float32)
    part_v = jnp.einsum("rm,rc->mc", mode_shapes[0], mass_rows, preferred_element_type=jnp.float32)
    proj_s, proj_v = lax.psum((part_s, part_v), "slab")
    eig_held = eigenvalues[0]
    eig_col = eig_held[:, None]
    first = (proj_s * lax.rsqrt(eig_col)).astype(jnp.bfloat16)
    second = (proj_s / eig_col - proj_v).astype(jnp.bfloat16)
    third = proj_v.astype(jnp.bfloat16)
    stacked = jnp.stack([first, second, third]).reshape(3, mode_count, adj_count, piece_width)
    my_slots = piece_slot[adjacency[sub_pos]]
    owner_hot = (
        my_slots[None, :] // owned_count == lax.iota(jnp.int32, sub_count)[:, None]
    ).astype(jnp.bfloat16)
    outgoing = jnp.einsum(
        "oa,kmab->okmb", owner_hot, stacked, preferred_element_type=jnp.float32
    ).astype(jnp.bfloat16)
    incoming = lax.all_to_all(outgoing, "sub", split_axis=0, concat_axis=0, tiled=True)
    all_slots = piece_slot[adjacency]
    targets = sub_pos * owned_count + lax.iota(jnp.int32, owned_count)
    select = jnp.any(all_slots[:, :, None] == targets[None, None, :], axis=1).astype(jnp.bfloat16)

    def piece_gram(weights):
        picked = incoming * weights[:, None, None, None]
        left_side = lax.dynamic_slice_in_dim(picked, slab_pos * quarter_rows, quarter_rows, 3)
        gram_stiff = jnp.einsum(
            "smb,smc->bc", left_side[:, 0], incoming[:, 0], preferred_element_type=jnp.float32
        )
        gram_mass = jnp.einsum(
            "smb,smc->bc", left_side[:, 1], incoming[:, 1], preferred_element_type=jnp.float32
        )
        gram_mass = gram_mass - jnp.einsum(
            "smb,smc->bc", left_side[:, 2], incoming[:, 2], preferred_element_type=jnp.float32
        )
        return (gram_stiff, gram_mass)

    gram_k, gram_m = lax.map(piece_gram, select.T)
    return (interface_k + gram_k, interface_m + gram_m)


def body(subs, slabs, *arrays):
    adjacency = arrays[5]
    if adjacency.shape[1] == subs and subs % slabs == 0:
        return dense_body(subs, slabs, *arrays)
    return sparse_body(*arrays)


def solution(mesh):
    placed = (
        P("sub", "slab", None),
        P("sub", "slab", None),
        P("sub", "slab", None),
        P("sub", None, None),
        P("sub", None),
        P(),
        P(),
        P("sub", "slab", None),
        P("sub", "slab", None),
    )
    return jax.shard_map(
        functools.partial(body, mesh.shape["sub"], mesh.shape["slab"]),
        mesh=mesh,
        in_specs=placed,
        out_specs=(P("sub", "slab", None), P("sub", "slab", None)),
        check_vma=False,
    )
```
